32 devices in a mesh: dp: 16 (over z, y, x), mp: 2 (over core).
Axes of the slice: x: 2, y: 2, z: 4, core: 2. Of those that a mesh axis runs over, the one named last changes fastest.
Arguments:
- pixels: bfloat16 [32, 512, 768], P(('dp', 'mp')), may hold values from -6 to 6
- counts: int32 [16, 2], P('dp'), may hold values from 128 to 512
- owner: int32 [16, 2], P('dp'), may hold values from 0 to 1, each once within a row
- embed_weight: bfloat16 [768, 1024], P('dp', 'mp'), may hold values from -0.21875 to 0.21875
- w_qkv: bfloat16 [3, 1024, 1024], P(None, 'dp', 'mp'), may hold values from -0.8 to 0.8
- w_out: bfloat16 [1024, 1024], P('mp', 'dp'), may hold values from -0.1875 to 0.1875
- w_up: bfloat16 [1024, 4096], P('dp', 'mp'), may hold values from -0.1875 to 0.1875
- w_down: bfloat16 [4096, 1024], P('mp', 'dp'), may hold values from -0.09375 to 0.09375
- ln1_gain: float32 [1024], replicated, may hold values from 0.25 to 1.75
- ln2_gain: float32 [1024], replicated, may hold values from 0.25 to 1.75
- targets: bfloat16 [16, 2, 512, 1024], P('dp', None, 'mp'), may hold values from -20 to 20
Outputs:
- encoded: bfloat16 [16, 2, 512, 1024], P('dp', None, 'mp')
- mean_loss: float32 [], replicated
The draws below stay inside these ranges and needn't reach their ends.
Inputs may be any that keep to these rules, and one draw needn't show every extreme that they name: counts[g, r] is the number of valid patches at the start of image g * 2 + r; the remaining patch slots are padding. Each row owner[g, :] is a permutation of 0 to 2 - 1, so every held image is encoded once.
All inputs are finite; a program needn't handle non-finite values.
Results may differ from the reference program's by a relative error of at most 0.014.
Values may be sent and summed in bfloat16 or wider, within the bound.
No kernel may reach another device: no remote copies, remote signals or barrier semaphores. Data moves between devices by JAX's collectives and lax.ppermute only.
A program may use at most 128 MiB of HBM per device.

```python
import math
import jax
import jax.numpy as jnp
from jax import lax

D = 1024
HEADS = 16
HEAD = 64
FF = 4096
PIX = 768
PATCHES = 512
IMAGES = 32
N_DP = 16
N_MP = 2


def draw_w_qkv(key, part):
    base = jax.random.normal(jax.random.fold_in(key, 11), (3, D, D), jnp.float32)
    stacked = base / math.sqrt(D)
    return jnp.clip(stacked, -0.78, 0.78).astype(jnp.bfloat16)


def draw_targets(key, part):
    place = jnp.arange(N_DP, dtype=jnp.float32) / max(N_DP - 1, 1)
    values = jax.random.normal(jax.random.fold_in(key, 22), (N_DP, N_MP, PATCHES, D), jnp.float32)
    scale = 0.5 + 2.0 * place
    return jnp.clip(values * scale[:, None, None, None], -20.0, 20.0).astype(jnp.bfloat16)


def place_ends(values, own_key, smallest, top_value):
    spot = [jax.random.randint(jax.random.fold_in(own_key, axis), (), 0, length) for axis, length in enumerate(values.shape)]
    longest = values.shape.index(max(values.shape))
    next_to = spot[:longest] + [(spot[longest] + 1) % values.shape[longest]] + spot[longest + 1:]
    return values.at[tuple(spot)].set(smallest).at[tuple(next_to)].set(top_value)


def steps_of(stream_key, extent, shards, smallest, high):
    def one(dim, shards_of):
        steps = jax.random.uniform(jax.random.fold_in(jax.random.fold_in(stream_key, 6), dim), (shards_of,), jnp.float32, smallest / len(shards), high / len(shards))
        return jnp.repeat(jnp.exp(steps), extent[dim] // shards_of).reshape((-1,) + (1,) * (len(extent) - dim - 1))

    gain = one(*shards[0])
    for cut in shards[1:]:
        gain = gain * one(*cut)
    return gain


def scatter_about(own_key, shape, deviation, bound, pieces=(), kind=jnp.bfloat16):
    result = jax.random.normal(own_key, shape, jnp.float32) * deviation
    if len(pieces) > 0:
        result = steps_of(own_key, shape, pieces, -0.22, 0.18) * result
    return jnp.clip(result, min=-bound, max=bound).astype(kind)


def setup_inputs(seed: int = 0) -> dict:
    splits = jax.random.split(jax.random.key(seed), 12)
    return {
        "pixels": scatter_about(splits[0], (IMAGES, PATCHES, PIX), 1.0, 6.0, ((0, 32),)),
        "counts": place_ends(jax.random.randint(splits[1], (N_DP, N_MP), PATCHES // 4, PATCHES + 1), jax.random.fold_in(splits[1], 1), PATCHES // 4, PATCHES).astype(jnp.int32),
        "owner": jax.vmap(lambda own: jax.random.permutation(own, N_MP))(jax.random.split(splits[2], N_DP)).reshape((N_DP, N_MP)).astype(jnp.int32),
        "embed_weight": scatter_about(splits[3], (PIX, D), PIX ** -0.5, 0.21875, ((0, 16), (1, 2))),
        "w_qkv": draw_w_qkv(jax.random.fold_in(splits[11], 71), 0),
        "w_out": scatter_about(splits[5], (D, D), D ** -0.5, 0.1875, ((0, 2), (1, 16))),
        "w_up": scatter_about(splits[6], (D, FF), D ** -0.5, 0.1875, ((0, 16), (1, 2))),
        "w_down": scatter_about(splits[7], (FF, D), FF ** -0.5, 0.09375, ((0, 2), (1, 16))),
        "ln1_gain": jnp.clip(1.0 + 0.15 * jax.random.normal(splits[8], (D,), jnp.float32), 0.25, 1.75),
        "ln2_gain": jnp.clip(1.0 + 0.15 * jax.random.normal(splits[9], (D,), jnp.float32), 0.25, 1.75),
        "targets": draw_targets(jax.random.fold_in(splits[11], 71), 0),
    }


def layer_norm(inputs, gains):
    average = lax.optimization_barrier(jnp.mean(inputs, axis=-1, keepdims=True))
    centred = inputs - average
    spread = lax.optimization_barrier(jnp.mean(centred * centred, axis=-1, keepdims=True))
    return centred * lax.rsqrt(spread + 1e-06) * gains.astype(jnp.float32)

def group_sum(left_mat, right_mat, groups):
    row_count = left_mat.shape[0]
    column_width = left_mat.shape[1] // groups
    left_part = left_mat.reshape(row_count, groups, column_width).astype(jnp.float32)
    right_part = right_mat.reshape(groups, column_width, right_mat.shape[1]).astype(jnp.float32)
    partial_value = jnp.einsum('pgh,ghd->gpd', left_part, right_part).astype(jnp.bfloat16)
    partial_value = lax.optimization_barrier(partial_value)
    return lax.optimization_barrier(jnp.sum(partial_value.astype(jnp.float32), axis=0))

def encode_image(picture, length, wanted, embed_weight, w_qkv, w_out, w_up, w_down, ln1_gain, ln2_gain):
    tokens = jnp.dot(picture, embed_weight, preferred_element_type=jnp.float32).astype(jnp.bfloat16)
    normed = layer_norm(tokens.astype(jnp.float32), ln1_gain).astype(jnp.bfloat16)
    factor = HEAD ** (-0.5)
    queries = (jnp.dot(normed, w_qkv[0], preferred_element_type=jnp.float32) * factor).astype(jnp.bfloat16)
    key_rows = jnp.dot(normed, w_qkv[1], preferred_element_type=jnp.float32).astype(jnp.bfloat16)
    value_rows = jnp.dot(normed, w_qkv[2], preferred_element_type=jnp.float32).astype(jnp.bfloat16)
    queries = queries.reshape(PATCHES, HEADS, HEAD)
    key_rows = key_rows.reshape(PATCHES, HEADS, HEAD)
    value_rows = value_rows.reshape(PATCHES, HEADS, HEAD)
    scores = jnp.einsum('qhd,khd->hqk', queries.astype(jnp.float32), key_rows.astype(jnp.float32))
    usable = jnp.arange(PATCHES, dtype=jnp.int32) < length
    scores = jnp.where(usable[None, None, :], scores, -1e+30)
    row_max = lax.optimization_barrier(jnp.max(scores, axis=-1, keepdims=True))
    expo = jnp.exp(scores - row_max)
    row_sum = lax.optimization_barrier(jnp.sum(expo, axis=-1))
    probs = lax.optimization_barrier(expo.astype(jnp.bfloat16))
    mixture = jnp.einsum('hqk,khd->qhd', probs.astype(jnp.float32), value_rows.astype(jnp.float32))
    mixture = mixture / jnp.transpose(row_sum)[:, :, None]
    attended = mixture.astype(jnp.bfloat16).reshape(PATCHES, D)
    residual = tokens.astype(jnp.float32) + group_sum(attended, w_out, N_MP)
    normed_two = layer_norm(residual, ln2_gain).astype(jnp.bfloat16)
    hidden = jax.nn.gelu(jnp.dot(normed_two, w_up, preferred_element_type=jnp.float32), approximate=False).astype(jnp.bfloat16)
    output = residual + group_sum(hidden, w_down, N_MP)
    misfit = output - wanted.astype(jnp.float32)
    squares = jnp.sum(jnp.where(usable[:, None], misfit * misfit, 0.0))
    number = jnp.sum(usable.astype(jnp.float32))
    return (output.astype(jnp.bfloat16), squares, number)

def reference(pixels, counts, owner, embed_weight, w_qkv, w_out, w_up, w_down, ln1_gain, ln2_gain, targets):
    order = owner.astype(jnp.int32)
    image_ids = (jnp.arange(N_DP, dtype=jnp.int32)[:, None] * N_MP + order).reshape(-1)
    lengths = jnp.take_along_axis(counts.astype(jnp.int32), order, axis=1).reshape(-1)
    wanted_all = targets.reshape(N_DP * N_MP, PATCHES, D)

    def encode_group(inputs):
        index, length, wanted = inputs
        picture = lax.dynamic_index_in_dim(pixels, index, 0, keepdims=False)
        return encode_image(picture, length, wanted, embed_weight, w_qkv, w_out, w_up, w_down, ln1_gain, ln2_gain)
    encoded, squares, number = lax.map(encode_group, (image_ids, lengths, wanted_all))
    mean_loss = jnp.sum(squares) / (D * jnp.sum(number))
    return (encoded.reshape(N_DP, N_MP, PATCHES, D), mean_loss)
```

```python
import functools

import jax
import jax.numpy as jnp
from jax import lax
from jax.experimental import pallas as pl
from jax.experimental.pallas import tpu as pltpu
from jax.sharding import PartitionSpec as P

HEAD = 64
TILE = 16
Z, Y, X = 0, 1, 2
MIB = 1 << 20
POS_Z, POS_Y, POS_X, POS_M, POS_LEN, POS_STEP = 0, 1, 2, 3, 4, 6


def ring_dims(count):
    nz = 4 if count % 4 == 0 else 1
    nx = 1
    while nx * nx < count // nz:
        nx *= 2
    ny = count // nz // nx
    return (nz, ny, nx) if nz * ny * nx == count else (1, 1, count)


def shift(value, dims, axis):
    pairs = []
    for z in range(dims[0]):
        for y in range(dims[1]):
            for x in range(dims[2]):
                to = [z, y, x]
                to[axis] = (to[axis] + 1) % dims[axis]
                pairs.append(
                    ((z * dims[1] + y) * dims[2] + x, (to[0] * dims[1] + to[1]) * dims[2] + to[2])
                )
    return lax.ppermute(value, "dp", pairs)


class Chunk:
    def __init__(self, array, slots, half):
        self.array, self.slots, self.half = array, slots, half
        self.rows = array.shape[0] // len(slots)

    def moved(self, array, axis, by=1):
        slots = [tuple(v + by * (i == axis) for i, v in enumerate(s)) for s in self.slots]
        return Chunk(array, slots, self.half)

    def part(self, first, last):
        return Chunk(
            self.array[first * self.rows : last * self.rows], self.slots[first:last], self.half
        )


def joined(chunks):
    if len(chunks) == 1:
        return chunks[0]
    return Chunk(
        jnp.concatenate([c.array for c in chunks], 0), sum((c.slots for c in chunks), []), chunks[0].half
    )


def together(*lists):
    flat = [c for chunks in lists for c in chunks]
    arrays = lax.optimization_barrier(tuple(c.array for c in flat))
    for c, a in zip(flat, arrays, strict=True):
        c.array = a


def step(chunk, dims, axis):
    return chunk.moved(shift(chunk.array, dims, axis), axis)


def swap_columns(value):
    return lax.ppermute(value, "mp", [(0, 1), (1, 0)])


def pair_gather(first, up, down, cut, dims):
    nz = dims[0]
    half = up.shape[0] // 2
    low = nz // 2
    here = [(0, 0, 0)]
    blocks_a = [Chunk(first[:cut], here, 0)]
    blocks_b = [Chunk(first[cut:], here, 1)]

    z_now = shift(first, dims, Z)
    side_a = jnp.concatenate([up[:half], down[:half]], 0)
    side_b = jnp.concatenate([up[half:], down[half:]], 0)
    from_x = shift(side_a, dims, X)
    from_y = shift(side_b, dims, Y)
    z_now, from_x, from_y = lax.optimization_barrier((z_now, from_x, from_y))

    def whole(own, k):
        rows = slice(k * half, (k + 1) * half)
        return (
            [Chunk(own[:half], here, 0), Chunk(from_x[rows], [(0, 0, 1)], 0)],
            [Chunk(own[half:], here, 1), Chunk(from_y[rows], [(0, 1, 0)], 1)],
        )

    up_a, up_b = (joined(c) for c in whole(up, 0))
    down_a, down_b = (joined(c) for c in whole(down, 1))

    def add_z(value, far):
        blocks_a.append(Chunk(value[:cut], [(far, 0, 0)], 0))
        blocks_b.append(Chunk(value[cut:], [(far, 0, 0)], 1))

    add_z(z_now, 1)
    a1, b1 = joined(blocks_a[:low]), joined(blocks_b[:low])
    z_next = shift(z_now, dims, Z)
    a1x, b1y = step(a1, dims, X), step(b1, dims, Y)
    z_now, a1x.array, b1y.array, up_a.array, up_b.array, down_a.array, down_b.array = (
        lax.optimization_barrier(
            (z_next, a1x.array, b1y.array, up_a.array, up_b.array, down_a.array, down_b.array)
        )
    )
    add_z(z_now, 2)
    a1, b1 = joined([a1, a1x]), joined([b1, b1y])
    z_next = shift(z_now, dims, Z)
    a1y, b1x = step(a1, dims, Y), step(b1, dims, X)
    z_now, a1y.array, b1x.array = lax.optimization_barrier((z_next, a1y.array, b1x.array))
    add_z(z_now, 3)
    a2, b2 = joined(blocks_a[low:]), joined(blocks_b[low:])
    up_z = [joined([up_a, up_b])]
    down_z = [joined([down_a, down_b])]
    up_z.append(step(up_z[-1], dims, Z))
    a2x, b2y = step(a2, dims, X), step(b2, dims, Y)
    together([up_z[-1], a2x, b2y])
    a2, b2 = joined([a2, a2x]), joined([b2, b2y])
    up_z.append(step(up_z[-1], dims, Z))
    a2y, b2x = step(a2, dims, Y), step(b2, dims, X)
    together([up_z[-1], a2y, b2x])
    first_parts = [a1, a1y, b1, b1x, a2, a2y, b2, b2x]

    def ends(blocks):
        a = joined([c.part(0, 2) for c in blocks])
        b = joined([c.part(2, 4) for c in blocks])
        b.half = 1
        return a, b

    ua1, ub1 = ends(up_z[:low])
    up_z.append(step(up_z[-1], dims, Z))
    ua1y, ub1x = step(ua1, dims, Y), step(ub1, dims, X)
    together([up_z[-1], ua1y, ub1x])
    ua2, ub2 = ends(up_z[low:])
    down_z.append(step(down_z[-1], dims, Z))
    ua2y, ub2x = step(ua2, dims, Y), step(ub2, dims, X)
    together([down_z[-1], ua2y, ub2x])
    up_parts = [ua1, ua1y, ub1, ub1x, ua2, ua2y, ub2, ub2x]
    da1, db1 = ends(down_z[:low])
    down_z.append(step(down_z[-1], dims, Z))
    da1y, db1x = step(da1, dims, Y), step(db1, dims, X)
    together([down_z[-1], da1y, db1x])
    down_z.append(step(down_z[-1], dims, Z))
    together([down_z[-1]])
    da2, db2 = ends(down_z[low:])
    da2y, db2x = step(da2, dims, Y), step(db2, dims, X)
    return first_parts, up_parts, [[da1, da1y, db1, db1x], [da2, da2y, db2, db2x]]


def pieces_of(chunks, spans, segment):
    found = []
    for number, chunk in enumerate(chunks):
        first, last = spans[chunk.half]
        low, high = max(first, segment[0]), min(last, segment[1])
        if low < high:
            for i, slot in enumerate(chunk.slots):
                found.append((number, i * chunk.rows + low - first, high - low, slot, low - segment[0]))
    return found


def source(pos, slot, dims, z_first=None):
    z, y, x = (lax.rem(pos[i] - slot[i] + dims[i], dims[i]) for i in (0, 1, 2))
    if z_first is not None:
        z = slot[0] - z_first
    return (z * dims[1] + y) * dims[2] + x


def copies(pos, dims, refs, pieces, into, block, sems, first_sem=0, z_first=None):
    made = []
    for i, (number, row, rows, slot, offset) in enumerate(pieces):
        to = offset
        if slot is not None:
            to = pl.multiple_of(source(pos, slot, dims, z_first) * block + offset, TILE)
        made.append(
            pltpu.make_async_copy(
                refs[number].at[pl.ds(row, rows)], into.at[pl.ds(to, rows)], sems.at[first_sem + i]
            )
        )
    return made


def nt_dot(left, right):
    return lax.dot_general(left, right, (((1,), (1,)), ((), ())), preferred_element_type=jnp.float32)


def dot(left, right):
    return jnp.dot(left, right, preferred_element_type=jnp.float32)


def any_spec():
    return pl.BlockSpec(memory_space=pl.ANY)


def vmem_spec():
    return pl.BlockSpec(memory_space=pltpu.VMEM)


def smem_spec():
    return pl.BlockSpec(memory_space=pltpu.SMEM)


def limits(mib):
    return pltpu.CompilerParams(vmem_limit_bytes=mib * MIB)


def cost(flops, moved, exps=0):
    return pl.CostEstimate(flops=flops, bytes_accessed=moved, transcendentals=exps)


def embed_kernel(n, dims, pieces, block, pos, mine, other, *rest):
    refs, (tokens, weight, sems) = rest[:n], rest[n:]
    made = copies(pos, dims, refs, pieces, weight, block, sems)
    for c in made:
        c.start()
    for c in made:
        c.wait()
    tokens[0] = dot(mine[...], weight[...]).astype(tokens.dtype)
    tokens[1] = dot(other[...], weight[...]).astype(tokens.dtype)


def embed(pos, dims, mine, other, chunks, pieces, block, columns):
    patches, pixels = mine.shape
    n = len(chunks)
    return pl.pallas_call(
        functools.partial(embed_kernel, n, dims, pieces, block),
        out_shape=jax.ShapeDtypeStruct((2, patches, columns), mine.dtype),
        in_specs=[smem_spec(), vmem_spec(), vmem_spec()] + [any_spec()] * n,
        out_specs=vmem_spec(),
        scratch_shapes=[
            pltpu.VMEM((pixels, columns), mine.dtype),
            pltpu.SemaphoreType.DMA((len(pieces),)),
        ],
        compiler_params=limits(16),
        cost_estimate=cost(4 * patches * pixels * columns, 4 * MIB),
        name="embed",
    )(pos, mine, other, *chunks)


def attention_kernel(n, dims, pieces, block, pos, mine, recv, gain, *rest):
    refs = rest[:n]
    keep, send, wq, wk, wv, wo, normed, q, k, v, mixed, sems = rest[n:]
    weights = (wq, wk, wv, wo)
    made, at = [], 0
    for weight, part in zip(weights, pieces, strict=True):
        made.append(copies(pos, dims, refs, part, weight, block, sems, at))
        at += len(part)
    for group in made:
        for c in group:
            c.start()
    m = pos[POS_M]
    patches, columns = mine.shape[1:]
    rows_own = patches // 2
    width = 2 * columns
    for i in range(2):
        low = mine[i].astype(jnp.float32)
        high = recv[1 - i].astype(jnp.float32)
        average = (
            jnp.sum(low, axis=-1, keepdims=True) + jnp.sum(high, axis=-1, keepdims=True)
        ) / width
        low, high = low - average, high - average
        spread = (
            jnp.sum(low * low, axis=-1, keepdims=True) + jnp.sum(high * high, axis=-1, keepdims=True)
        ) / width
        scale = lax.rsqrt(spread + 1e-06)
        normed[i, 0] = (low * scale * gain[0:1]).astype(normed.dtype)
        normed[i, 1] = (high * scale * gain[1:2]).astype(normed.dtype)
    here = pl.ds(pl.multiple_of(m * columns, columns), columns)
    there = pl.ds(pl.multiple_of((1 - m) * columns, columns), columns)
    for weight, group, result, factor in zip(
        weights[:3], made[:3], (q, k, v), (HEAD**-0.5, 1.0, 1.0), strict=True
    ):
        for c in group:
            c.wait()
        for i in range(2):
            value = dot(normed[i, 0], weight[here, :]) + dot(normed[i, 1], weight[there, :])
            if factor != 1.0:
                value = value * factor
            result[i] = value.astype(result.dtype)
    pair = 2 * HEAD
    key_ids = lax.broadcasted_iota(jnp.int32, (1, patches), 1)
    lane = lax.broadcasted_iota(jnp.int32, (patches, pair), 1)
    first = lane < HEAD
    for i in range(2):
        masked = jnp.where(key_ids < pos[POS_LEN + i], 0.0, -1e30).astype(jnp.float32)
        for h in range(columns // pair):
            cut = slice(h * pair, (h + 1) * pair)
            q_pair, k_pair, v_pair = q[i, :, cut], k[i, :, cut], v[i, :, cut]
            found = []
            for own in (first, jnp.logical_not(first)):
                scores = nt_dot(q_pair, jnp.where(own, k_pair, jnp.zeros_like(k_pair))) + masked
                expo = jnp.exp(scores - jnp.max(scores, axis=-1, keepdims=True))
                value = dot(
                    expo.astype(v_pair.dtype), jnp.where(own, v_pair, jnp.ones_like(v_pair))
                )
                found.append(value / pltpu.roll(value, HEAD, 1))
            mixed[i, :, cut] = jnp.where(first, found[0], found[1]).astype(mixed.dtype)
    for c in made[3]:
        c.wait()
    own_rows = pl.ds(pl.multiple_of(m * rows_own, rows_own), rows_own)
    far_rows = pl.ds(pl.multiple_of((1 - m) * rows_own, rows_own), rows_own)
    for i in range(2):
        keep[i] = nt_dot(mixed[i, own_rows, :], wo[...]).astype(keep.dtype)
        send[i] = nt_dot(mixed[i, far_rows, :], wo[...]).astype(send.dtype)


def attention(pos, dims, mine, recv, gain, chunks, pieces, block, width):
    _, patches, columns = mine.shape
    n = len(chunks)
    kind = mine.dtype
    out = jax.ShapeDtypeStruct((2, patches // 2, width), kind)
    weight = pltpu.VMEM((width, columns), kind)
    whole = pltpu.VMEM((2, patches, columns), kind)
    return pl.pallas_call(
        functools.partial(attention_kernel, n, dims, pieces, block),
        out_shape=(out, out),
        in_specs=[smem_spec(), vmem_spec(), vmem_spec(), vmem_spec()] + [any_spec()] * n,
        out_specs=(vmem_spec(), vmem_spec()),
        scratch_shapes=[weight] * 4
        + [pltpu.VMEM((2, 2, patches, columns), kind)]
        + [whole] * 4
        + [pltpu.SemaphoreType.DMA((sum(len(p) for p in pieces),))],
        compiler_params=limits(32),
        cost_estimate=cost(
            2 * 2 * patches * width * columns * 4 + 8 * patches * patches * columns,
            10 * MIB,
            2 * patches * patches * columns // HEAD,
        ),
        name="attention",
    )(pos, mine, recv, gain, *chunks)


def residual_kernel(pos, mine, recv, keep, came, gain, residual, normed):
    m = pos[POS_M]
    columns = mine.shape[2]
    rows = keep.shape[1]
    width = 2 * columns
    own_rows = pl.ds(pl.multiple_of(m * rows, rows), rows)
    here = pl.ds(pl.multiple_of(m * columns, columns), columns)
    there = pl.ds(pl.multiple_of((1 - m) * columns, columns), columns)
    for i in range(2):
        parts = []
        for tokens, at in ((mine[i, own_rows, :], here), (recv[1 - i, own_rows, :], there)):
            parts.append(
                tokens.astype(jnp.float32)
                + (keep[i, :, at].astype(jnp.float32) + came[1 - i, :, at].astype(jnp.float32))
            )
            residual[i, :, at] = parts[-1]
        average = sum(jnp.sum(v, axis=-1, keepdims=True) for v in parts) / width
        parts = [v - average for v in parts]
        spread = sum(jnp.sum(v * v, axis=-1, keepdims=True) for v in parts) / width
        scale = lax.rsqrt(spread + 1e-06)
        for v, at in zip(parts, (here, there), strict=True):
            normed[i, :, at] = (v * scale * gain[0:1, at]).astype(normed.dtype)


def residual_and_norm(pos, mine, recv, keep, came, gain):
    return pl.pallas_call(
        residual_kernel,
        out_shape=(
            jax.ShapeDtypeStruct(keep.shape, jnp.float32),
            jax.ShapeDtypeStruct(keep.shape, keep.dtype),
        ),
        in_specs=[smem_spec()] + [vmem_spec()] * 5,
        out_specs=(vmem_spec(), vmem_spec()),
        compiler_params=limits(16),
        cost_estimate=cost(10 * keep.size, 10 * MIB),
        name="residual",
    )(pos, mine, recv, keep, came, gain)


def gelu(x):
    t = 1.0 / (1.0 + (0.3275911 * 0.7071067811865476) * jnp.abs(x))
    poly = 0.5 * 1.061405429
    for a in (-1.453152027, 1.421413741, -0.284496736, 0.254829592):
        poly = poly * t + 0.5 * a
    tail = poly * t * jnp.exp(-0.5 * (x * x))
    return x * jnp.where(x < 0.0, tail, 1.0 - tail)


def up_kernel(n, dims, pieces, block, pos, own, came, *rest):
    refs, (hidden, weight, sems) = rest[:n], rest[n:]
    made = copies(pos, dims, refs, pieces, weight, block, sems)
    for c in made:
        c.start()
    for c in made:
        c.wait()
    tile = 512
    for i in range(2):
        for j in range(hidden.shape[-1] // tile):
            at = slice(j * tile, (j + 1) * tile)
            for k, side in enumerate((own[i], came[1 - i])):
                hidden[k, i, :, at] = gelu(dot(side, weight[:, at])).astype(hidden.dtype)


def up_layer(pos, dims, own, came, chunks, pieces, block, units):
    _, rows, width = own.shape
    n = len(chunks)
    return pl.pallas_call(
        functools.partial(up_kernel, n, dims, pieces, block),
        out_shape=jax.ShapeDtypeStruct((2, 2, rows, units), own.dtype),
        in_specs=[smem_spec(), vmem_spec(), vmem_spec()] + [any_spec()] * n,
        out_specs=vmem_spec(),
        scratch_shapes=[
            pltpu.VMEM((width, units), own.dtype),
            pltpu.SemaphoreType.DMA((len(pieces),)),
        ],
        compiler_params=limits(24),
        cost_estimate=cost(8 * rows * width * units, 10 * MIB, 4 * rows * units),
        name="up",
    )(pos, own, came, *chunks)


def down_kernel(n, dims, pieces, block, z_first, pos, hidden, *rest):
    refs, (keep, send, weight, sems) = rest[:n], rest[n:]
    made = copies(pos, dims, refs, pieces, weight, block, sems, 0, z_first)
    for c in made:
        c.start()
    for c in made:
        c.wait()
    for i in range(2):
        for k, result in enumerate((keep, send)):
            result[i] = nt_dot(hidden[k, i], weight[...]).astype(result.dtype)


def down_layer(pos, dims, hidden, chunks, pieces, block, z_first, columns):
    _, _, rows, units = hidden.shape
    n = len(chunks)
    out = jax.ShapeDtypeStruct((2, rows, columns), hidden.dtype)
    return pl.pallas_call(
        functools.partial(down_kernel, n, dims, pieces, block, z_first),
        out_shape=(out, out),
        in_specs=[smem_spec(), vmem_spec()] + [any_spec()] * n,
        out_specs=(vmem_spec(), vmem_spec()),
        scratch_shapes=[
            pltpu.VMEM((columns, units), hidden.dtype),
            pltpu.SemaphoreType.DMA((len(pieces),)),
        ],
        compiler_params=limits(24),
        cost_estimate=cost(8 * rows * columns * units, 8 * MIB),
        name="down",
    )(pos, hidden, *chunks)


def output_kernel(n, nz, starts, pos, residual, targets, *rest):
    parts, (encoded, squares) = rest[:n], rest[n:]
    m = pos[POS_M]
    rows = residual.shape[1]
    total = jnp.zeros((), jnp.float32)
    row_ids = m * rows + lax.broadcasted_iota(jnp.int32, (rows, 1), 0)
    for i in range(2):
        s = pos[POS_STEP] if i == 0 else 1 - pos[POS_STEP]
        usable = row_ids < pos[POS_LEN + i]
        sums = jnp.zeros((rows, 1), jnp.float32)
        for j, spots in enumerate(starts):
            keep, came = parts[2 * j], parts[2 * j + 1]
            size = keep.shape[2] // len(spots)
            for b, back in enumerate(spots):
                at = slice(b * size, (b + 1) * size)
                if back is None:
                    place = pl.ds(0, size)
                else:
                    begin = lax.rem(pos[POS_Z] - back + nz, nz) * size
                    place = pl.ds(pl.multiple_of(begin, size), size)
                value = residual[i, :, place] + (
                    keep[i, :, at].astype(jnp.float32) + came[1 - i, :, at].astype(jnp.float32)
                )
                encoded[s, :, place] = value.astype(encoded.dtype)
                misfit = value - targets[s, :, place].astype(jnp.float32)
                sums = sums + jnp.sum(misfit * misfit, axis=-1, keepdims=True)
        total = total + jnp.sum(jnp.where(usable, sums, 0.0))
    squares[...] = jnp.full(squares.shape, total, jnp.float32)


def output_layer(pos, residual, targets, nz, starts, parts):
    return pl.pallas_call(
        functools.partial(output_kernel, len(parts), nz, starts),
        out_shape=(
            jax.ShapeDtypeStruct(residual.shape, targets.dtype),
            jax.ShapeDtypeStruct((8, 128), jnp.float32),
        ),
        in_specs=[smem_spec()] + [vmem_spec()] * (2 + len(parts)),
        out_specs=(vmem_spec(), vmem_spec()),
        compiler_params=limits(24),
        cost_estimate=cost(8 * residual.size, 8 * MIB),
        name="output",
    )(pos, residual, targets, *parts)


def on_device(
    pixels, counts, owner, embed_weight, w_qkv, w_out, w_up, w_down, ln1_gain, ln2_gain, targets
):
    picture = pixels[0]
    devices, cores = lax.axis_size("dp"), lax.axis_size("mp")
    assert cores == 2
    index, m = lax.axis_index("dp"), lax.axis_index("mp")
    dims = ring_dims(devices)
    width = ln1_gain.shape[0]
    columns = width // cores
    lengths, order = counts[0], owner[0]
    length_mine = jnp.where(m == 0, lengths[0], lengths[1])
    length_other = jnp.where(m == 0, lengths[1], lengths[0])
    step_mine = jnp.where(order[0] == m, 0, 1)
    pos = jnp.stack(
        [
            index // (dims[1] * dims[2]),
            index // dims[2] % dims[1],
            index % dims[2],
            m,
            length_mine,
            length_other,
            step_mine,
            jnp.zeros_like(m),
        ]
    ).astype(jnp.int32)
    gain_halves = ln1_gain.reshape(cores, columns)
    gain_one = jnp.where(m == 0, gain_halves, gain_halves[::-1])

    shards = [embed_weight, w_qkv[0], w_qkv[1], w_qkv[2], w_out.T]
    up, down = w_up, w_down.T
    block, block_e = up.shape[0], embed_weight.shape[0]
    total = sum(s.shape[0] for s in shards)
    cut = total // 2 // TILE * TILE
    in_slots = (
        dims[0] == 4
        and dims[1] == 2
        and dims[2] == 2
        and block % (2 * TILE) == 0
        and block_e % TILE == 0
    )
    other_picture = swap_columns(picture)
    if in_slots:
        first_parts, up_parts, down_parts = pair_gather(
            jnp.concatenate(shards, 0), up, down, cut, dims
        )
        spans = ((0, cut), (cut, total))
        halves = ((0, block // 2), (block // 2, block))
        bounds = [0]
        for s in shards:
            bounds.append(bounds[-1] + s.shape[0])
        first_pieces = [
            pieces_of(first_parts, spans, (bounds[i], bounds[i + 1])) for i in range(len(shards))
        ]
        up_pieces = pieces_of(up_parts, halves, (0, block))
        down_pieces = [pieces_of(part, halves, (0, block)) for part in down_parts]
        starts = [sorted({p[3][0] for p in pieces}) for pieces in down_pieces]
    else:
        gathered = [lax.all_gather(s, "dp", axis=0, tiled=True) for s in (*shards, up, down)]
        whole = [Chunk(g, [None], 0) for g in gathered]
        first_parts, up_parts, down_parts = whole[:5], whole[5:6], [whole[6:]]
        first_pieces = [[(i, 0, c.rows, None, 0)] for i, c in enumerate(first_parts)]
        up_pieces = [(0, 0, up_parts[0].rows, None, 0)]
        down_pieces = [[(0, 0, down_parts[0][0].rows, None, 0)]]
        starts = [[None]]

    first_arrays = [c.array for c in first_parts]
    embed_at = sorted({p[0] for p in first_pieces[0]})
    embed_pieces = [(embed_at.index(p[0]), *p[1:]) for p in first_pieces[0]]
    mine = embed(
        pos, dims, picture, other_picture, [first_arrays[i] for i in embed_at], embed_pieces, block_e, columns
    )
    recv = swap_columns(mine)
    keep, send = attention(
        pos, dims, mine, recv, gain_one, first_arrays, first_pieces[1:], block, width
    )
    came = swap_columns(send)
    residual, normed = residual_and_norm(
        pos, mine, recv, keep, came, ln2_gain.reshape(1, width)
    )
    normed_came = swap_columns(normed)
    hidden = up_layer(
        pos, dims, normed, normed_came, [c.array for c in up_parts], up_pieces, block, up.shape[1]
    )
    finals = []
    for part, pieces, spots in zip(down_parts, down_pieces, starts, strict=True):
        kept, sent = down_layer(
            pos, dims, hidden, [c.array for c in part], pieces, block, spots[0], width // len(down_parts)
        )
        finals += [kept, swap_columns(sent)]
    encoded, squares = output_layer(pos, residual, targets[0], dims[0], starts, finals)
    number = jnp.sum(lengths).astype(jnp.float32) / cores
    mine_sums = jnp.stack([squares[0, 0], number])
    sums = lax.all_to_all(
        jnp.broadcast_to(mine_sums[None, None, :], (devices * cores, 1, 2)), ("dp", "mp"), 0, 0, tiled=True
    )
    total_squares, total_number = jnp.sum(sums, axis=(0, 1))
    return (encoded[None], total_squares / (width * total_number))


def solution(mesh):
    in_specs = (
        P(("dp", "mp"), None, None),
        P("dp", None),
        P("dp", None),
        P("dp", "mp"),
        P(None, "dp", "mp"),
        P("mp", "dp"),
        P("dp", "mp"),
        P("mp", "dp"),
        P(),
        P(),
        P("dp", None, "mp", None),
    )
    out_specs = (P("dp", None, "mp", None), P())
    return jax.shard_map(
        on_device, mesh=mesh, in_specs=in_specs, out_specs=out_specs, check_vma=False
    )
```

```python
import functools

import jax
import jax.numpy as jnp
from jax import lax
from jax.experimental import pallas as pl
from jax.experimental.pallas import tpu as pltpu
from jax.sharding import PartitionSpec as P

HEAD = 64
TILE = 16
Z, Y, X = 0, 1, 2
MIB = 1 << 20
POS_Z, POS_Y, POS_X, POS_M, POS_LEN, POS_STEP = 0, 1, 2, 3, 4, 6


def ring_dims(count):
    nz = 4 if count % 4 == 0 else 1
    nx = 1
    while nx * nx < count // nz:
        nx *= 2
    ny = count // nz // nx
    return (nz, ny, nx) if nz * ny * nx == count else (1, 1, count)


def shift(value, dims, *axes):
    pairs = []
    for z in range(dims[0]):
        for y in range(dims[1]):
            for x in range(dims[2]):
                to = [z, y, x]
                for axis in axes:
                    to[axis] = (to[axis] + 1) % dims[axis]
                pairs.append(
                    ((z * dims[1] + y) * dims[2] + x, (to[0] * dims[1] + to[1]) * dims[2] + to[2])
                )
    return lax.ppermute(value, "dp", pairs)


class Chunk:
    def __init__(self, array, slots, half):
        self.array, self.slots, self.half = array, slots, half
        self.rows = array.shape[0] // len(slots)

    def moved(self, array, axis, by=1):
        slots = [tuple(v + by * (i == axis) for i, v in enumerate(s)) for s in self.slots]
        return Chunk(array, slots, self.half)

    def part(self, first, last):
        return Chunk(
            self.array[first * self.rows : last * self.rows], self.slots[first:last], self.half
        )


    def without(self, rows, half):
        value = self.array.reshape(len(self.slots), self.rows, -1)[:, rows:]
        return Chunk(value.reshape(-1, value.shape[2]), self.slots, half)


def joined(chunks):
    if len(chunks) == 1:
        return chunks[0]
    return Chunk(
        jnp.concatenate([c.array for c in chunks], 0), sum((c.slots for c in chunks), []), chunks[0].half
    )


def swap_columns(value):
    return lax.ppermute(value, "mp", [(0, 1), (1, 0)])


class Gather:
    def __init__(self, first, up, down, side_a, side_b, spans, dims):
        self.dims, self.spans, self.half = dims, spans, up.shape[0] // 2
        self.first, self.up, self.down, self.side_a, self.side_b = first, up, down, side_a, side_b

    def move(self, value, axis):
        return shift(value, self.dims, axis)

    def step(self, chunk, axis):
        return chunk.moved(shift(chunk.array, self.dims, axis), axis)

    def first_ends(self, blocks, low, kinds):
        slots = [(low + i, 0, 0) for i in range(len(blocks))]
        made = []
        for kind in kinds:
            begin, end = self.spans[kind]
            made.append(Chunk(jnp.concatenate([v[begin:end] for v in blocks], 0), slots, kind))
        return made

    def whole(self, shard, k):
        half = self.half
        rows = slice(k * half, (k + 1) * half)
        here = [(0, 0, 0)]
        return joined(
            [
                Chunk(shard[:half], here, 0),
                Chunk(self.from_x[rows], [(0, 0, 1)], 0),
                Chunk(shard[half:], here, 1),
                Chunk(self.from_y[rows], [(0, 1, 0)], 1),
            ]
        )

    def halves(self, blocks):
        a = joined([c.part(0, 2) for c in blocks])
        b = joined([c.part(2, 4) for c in blocks])
        b.half = 1
        return a, b

    def slot(self, number):
        if number == 0:
            self.first_z = [self.first, self.move(self.first, Z)]
            self.from_x, self.from_y = self.move(self.side_a, X), self.move(self.side_b, Y)
        elif number == 1:
            self.first_z.append(self.move(self.first_z[-1], Z))
            self.a, self.b = self.first_ends(self.first_z[:2], 0, (0, 1))
            self.a_far, self.b_far = self.step(self.a, X), self.step(self.b, Y)
            self.up_z, self.down_z = [self.whole(self.up, 0)], [self.whole(self.down, 1)]
        elif number == 2:
            self.first_z.append(self.move(self.first_z[-1], Z))
            self.a, self.b = joined([self.a, self.a_far]), joined([self.b, self.b_far])
            self.parts = [self.a, self.step(self.a, Y), self.b, self.step(self.b, X)]
        elif number == 3:
            self.up_z.append(self.step(self.up_z[-1], Z))
            self.a, self.b, own = self.first_ends(self.first_z[2:], 2, (5, 3, 4))
            corner = Chunk(shift(own.array, self.dims, X, Y), [(z, 1, 1) for z, _, _ in own.slots], 4)
            self.a_far = self.step(self.a, X)
            rows = self.b.array.shape[0]
            mixed = self.move(jnp.concatenate([self.b.array, own.array], 0), Y)
            self.b_far, own_far = self.b.moved(mixed[:rows], Y), own.moved(mixed[rows:], Y)
            self.early = self.parts[:2] + [self.a, self.a_far, own_far, corner]
        elif number == 4:
            self.up_z.append(self.step(self.up_z[-1], Z))
            self.a, self.b = joined([self.a, self.a_far]), joined([self.b, self.b_far])
            self.a = self.a.without(self.spans[5][1] - self.spans[2][1] + self.spans[2][0], 2)
            self.parts += [self.a, self.step(self.a, Y), self.b, self.step(self.b, X)]
        elif number == 5:
            self.up_parts = self.last(self.up_z[:2])
            self.up_z.append(self.step(self.up_z[-1], Z))
        elif number == 6:
            self.up_parts += self.last(self.up_z[2:])
            self.down_z.append(self.step(self.down_z[-1], Z))
        elif number == 7:
            self.down_parts = [self.last(self.down_z[:2])]
            self.down_z.append(self.step(self.down_z[-1], Z))
        elif number == 8:
            self.down_z.append(self.step(self.down_z[-1], Z))
            self.down_parts.append(self.last(self.down_z[2:3]))
        elif number == 9:
            self.down_parts.append(self.last(self.down_z[3:]))

    def last(self, blocks):
        a, b = self.halves(blocks)
        return [a, self.step(a, Y), b, self.step(b, X)]

    def end_slot(self, *others):
        chunks, arrays = [], []
        for name, value in vars(self).items():
            for i, v in enumerate(value if isinstance(value, list) else [value]):
                for k, w in enumerate(v if isinstance(v, list) else [v]):
                    if isinstance(w, Chunk):
                        if all(w is not c for c in chunks):
                            chunks.append(w)
                    elif isinstance(w, jax.Array):
                        arrays.append((name, i, w))
        together = lax.optimization_barrier(
            (tuple(c.array for c in chunks), tuple(w for _, _, w in arrays), others)
        )
        for c, new in zip(chunks, together[0], strict=True):
            c.array = new
        for (name, i, _), new in zip(arrays, together[1], strict=True):
            if isinstance(vars(self)[name], list):
                vars(self)[name][i] = new
            else:
                setattr(self, name, new)
        return together[2]


def pieces_of(chunks, spans, segment):
    found = []
    for number, chunk in enumerate(chunks):
        first, last = spans[chunk.half]
        low, high = max(first, segment[0]), min(last, segment[1])
        if low < high:
            for i, slot in enumerate(chunk.slots):
                found.append((number, i * chunk.rows + low - first, high - low, slot, low - segment[0]))
    return found


def source(pos, slot, dims, z_first=None):
    z, y, x = (lax.rem(pos[i] - slot[i] + dims[i], dims[i]) for i in (0, 1, 2))
    if z_first is not None:
        z = slot[0] - z_first
    return (z * dims[1] + y) * dims[2] + x


def lay_out(pos, dims, refs, pieces, into, block, z_first=None):
    for number, row, rows, slot, offset in pieces:
        to = offset
        if slot is not None:
            to = pl.multiple_of(source(pos, slot, dims, z_first) * block + offset, TILE)
        into[pl.ds(to, rows), :] = refs[number][pl.ds(row, rows), :]


def nt_dot(left, right):
    return lax.dot_general(left, right, (((1,), (1,)), ((), ())), preferred_element_type=jnp.float32)


def dot(left, right):
    return jnp.dot(left, right, preferred_element_type=jnp.float32)


def any_spec():
    return pl.BlockSpec(memory_space=pl.ANY)


def hbm_spec():
    return pl.BlockSpec(memory_space=pltpu.HBM)


def vmem_spec():
    return pl.BlockSpec(memory_space=pltpu.VMEM)


def smem_spec():
    return pl.BlockSpec(memory_space=pltpu.SMEM)


def limits(mib):
    return pltpu.CompilerParams(vmem_limit_bytes=mib * MIB)


def cost(flops, moved, exps=0):
    return pl.CostEstimate(flops=0, bytes_accessed=1024, transcendentals=0)


def pack_kernel(*rest):
    *shards, up, down, first, side_a, side_b, sems = rest
    half = up.shape[0] // 2
    moves, at = [], 0
    for shard in shards:
        for part in [shard] if len(shard.shape) == 2 else [shard.at[i] for i in range(shard.shape[0])]:
            moves.append((part, first.at[pl.ds(at, part.shape[0])]))
            at += part.shape[0]
    for k, shard in enumerate((up, down)):
        moves.append((shard.at[pl.ds(0, half)], side_a.at[pl.ds(k * half, half)]))
        moves.append((shard.at[pl.ds(half, half)], side_b.at[pl.ds(k * half, half)]))
    made = [pltpu.make_async_copy(a, b, sems.at[i]) for i, (a, b) in enumerate(moves)]
    for c in made:
        c.start()
    for c in made:
        c.wait()


def pack(shards, up, down):
    rows = sum(s.size for s in shards) // shards[0].shape[1]
    first = jax.ShapeDtypeStruct((rows, shards[0].shape[1]), up.dtype)
    side = jax.ShapeDtypeStruct(up.shape, up.dtype)
    return pl.pallas_call(
        pack_kernel,
        out_shape=(first, side, side),
        in_specs=[hbm_spec()] * (len(shards) + 2),
        out_specs=(vmem_spec(),) * 3,
        scratch_shapes=[pltpu.SemaphoreType.DMA((rows // shards[0].shape[0] + 4,))],
        compiler_params=limits(60),
        cost_estimate=cost(0, 2 * MIB),
        name="pack",
    )(*shards, up, down)


def pack_order(packed, up, down):
    first, side_a, side_b = packed
    return first, up, down, side_a, side_b


def embed_kernel(n, dims, pieces, block, pos, mine, other, *rest):
    refs, (tokens, weight) = rest[:n], rest[n:]
    lay_out(pos, dims, refs, pieces, weight, block)
    tokens[0] = dot(mine[...], weight[...]).astype(tokens.dtype)
    tokens[1] = dot(other[...], weight[...]).astype(tokens.dtype)


def embed(pos, dims, mine, other, chunks, pieces, block, columns):
    patches, pixels = mine.shape
    n = len(chunks)
    return pl.pallas_call(
        functools.partial(embed_kernel, n, dims, pieces, block),
        out_shape=jax.ShapeDtypeStruct((2, patches, columns), mine.dtype),
        in_specs=[smem_spec(), vmem_spec(), vmem_spec()] + [vmem_spec()] * n,
        out_specs=vmem_spec(),
        scratch_shapes=[pltpu.VMEM((pixels, columns), mine.dtype)],
        compiler_params=limits(8),
        cost_estimate=cost(4 * patches * pixels * columns, 4 * MIB),
        name="embed",
    )(pos, mine, other, *chunks)


def project_kernel(n, dims, pieces, block, pos, mine, recv, gain, *rest):
    refs = rest[:n]
    q, k, v, weight, normed = rest[n:]
    m = pos[POS_M]
    columns = mine.shape[2]
    width = 2 * columns
    for i in range(2):
        low = mine[i].astype(jnp.float32)
        high = recv[1 - i].astype(jnp.float32)
        average = (
            jnp.sum(low, axis=-1, keepdims=True) + jnp.sum(high, axis=-1, keepdims=True)
        ) / width
        low, high = low - average, high - average
        spread = (
            jnp.sum(low * low, axis=-1, keepdims=True) + jnp.sum(high * high, axis=-1, keepdims=True)
        ) / width
        scale = lax.rsqrt(spread + 1e-06)
        normed[i, 0] = (low * scale * gain[0:1]).astype(normed.dtype)
        normed[i, 1] = (high * scale * gain[1:2]).astype(normed.dtype)
    here = pl.ds(pl.multiple_of(m * columns, columns), columns)
    there = pl.ds(pl.multiple_of((1 - m) * columns, columns), columns)
    for some, result, factor in zip(pieces, (q, k, v), (HEAD**-0.5, 1.0, 1.0), strict=True):
        lay_out(pos, dims, refs, some, weight, block)
        for i in range(2):
            value = dot(normed[i, 0], weight[here, :]) + dot(normed[i, 1], weight[there, :])
            if factor != 1.0:
                value = value * factor
            result[i] = value.astype(result.dtype)


def project(pos, dims, mine, recv, gain, chunks, pieces, block, width):
    _, patches, columns = mine.shape
    n = len(chunks)
    kind = mine.dtype
    out = jax.ShapeDtypeStruct(mine.shape, kind)
    return pl.pallas_call(
        functools.partial(project_kernel, n, dims, pieces, block),
        out_shape=(out, out, out),
        in_specs=[smem_spec(), vmem_spec(), vmem_spec(), vmem_spec()] + [vmem_spec()] * n,
        out_specs=(vmem_spec(),) * 3,
        scratch_shapes=[
            pltpu.VMEM((width, columns), kind),
            pltpu.VMEM((2, 2, patches, columns), kind),
        ],
        compiler_params=limits(11),
        cost_estimate=cost(2 * 2 * patches * width * columns * 3, 8 * MIB),
        name="project",
    )(pos, mine, recv, gain, *chunks)


def attention_kernel(n, dims, pieces, block, pos, q, k, v, *rest):
    refs = rest[:n]
    keep, send, wo, mixed = rest[n:]
    lay_out(pos, dims, refs, pieces, wo, block)
    m = pos[POS_M]
    patches, columns = q.shape[1:]
    rows_own = patches // 2
    pair = 2 * HEAD
    key_ids = lax.broadcasted_iota(jnp.int32, (1, patches), 1)
    lane = lax.broadcasted_iota(jnp.int32, (patches, pair), 1)
    first = lane < HEAD
    for i in range(2):
        masked = jnp.where(key_ids < pos[POS_LEN + i], 0.0, -1e30).astype(jnp.float32)
        for h in range(columns // pair):
            cut = slice(h * pair, (h + 1) * pair)
            q_pair, k_pair, v_pair = q[i, :, cut], k[i, :, cut], v[i, :, cut]
            found = []
            for own in (first, jnp.logical_not(first)):
                scores = nt_dot(q_pair, jnp.where(own, k_pair, jnp.zeros_like(k_pair))) + masked
                expo = jnp.exp(scores - jnp.max(scores, axis=-1, keepdims=True))
                value = dot(
                    expo.astype(v_pair.dtype), jnp.where(own, v_pair, jnp.ones_like(v_pair))
                )
                found.append(value / pltpu.roll(value, HEAD, 1))
            mixed[i, :, cut] = jnp.where(first, found[0], found[1]).astype(mixed.dtype)
    own_rows = pl.ds(pl.multiple_of(m * rows_own, rows_own), rows_own)
    far_rows = pl.ds(pl.multiple_of((1 - m) * rows_own, rows_own), rows_own)
    for i in range(2):
        keep[i] = nt_dot(mixed[i, own_rows, :], wo[...]).astype(keep.dtype)
        send[i] = nt_dot(mixed[i, far_rows, :], wo[...]).astype(send.dtype)


def attention(pos, dims, q, k, v, chunks, pieces, block, width):
    _, patches, columns = q.shape
    n = len(chunks)
    out = jax.ShapeDtypeStruct((2, patches // 2, width), q.dtype)
    return pl.pallas_call(
        functools.partial(attention_kernel, n, dims, pieces, block),
        out_shape=(out, out),
        in_specs=[smem_spec()] + [vmem_spec()] * 3 + [vmem_spec()] * n,
        out_specs=(vmem_spec(), vmem_spec()),
        scratch_shapes=[
            pltpu.VMEM((width, columns), q.dtype),
            pltpu.VMEM(q.shape, q.dtype),
        ],
        compiler_params=limits(10),
        cost_estimate=cost(
            4 * patches * width * columns + 8 * patches * patches * columns,
            8 * MIB,
            2 * patches * patches * columns // HEAD,
        ),
        name="attention",
    )(pos, q, k, v, *chunks)


def residual_kernel(pos, mine, recv, keep, came, gain, residual, normed):
    m = pos[POS_M]
    columns = mine.shape[2]
    rows = keep.shape[1]
    width = 2 * columns
    own_rows = pl.ds(pl.multiple_of(m * rows, rows), rows)
    here = pl.ds(pl.multiple_of(m * columns, columns), columns)
    there = pl.ds(pl.multiple_of((1 - m) * columns, columns), columns)
    for i in range(2):
        parts = []
        for tokens, at in ((mine[i, own_rows, :], here), (recv[1 - i, own_rows, :], there)):
            parts.append(
                tokens.astype(jnp.float32)
                + (keep[i, :, at].astype(jnp.float32) + came[1 - i, :, at].astype(jnp.float32))
            )
            residual[i, :, at] = parts[-1]
        average = sum(jnp.sum(v, axis=-1, keepdims=True) for v in parts) / width
        parts = [v - average for v in parts]
        spread = sum(jnp.sum(v * v, axis=-1, keepdims=True) for v in parts) / width
        scale = lax.rsqrt(spread + 1e-06)
        for v, at in zip(parts, (here, there), strict=True):
            normed[i, :, at] = (v * scale * gain[0:1, at]).astype(normed.dtype)


def residual_and_norm(pos, mine, recv, keep, came, gain):
    return pl.pallas_call(
        residual_kernel,
        out_shape=(
            jax.ShapeDtypeStruct(keep.shape, jnp.float32),
            jax.ShapeDtypeStruct(keep.shape, keep.dtype),
        ),
        in_specs=[smem_spec()] + [vmem_spec()] * 5,
        out_specs=(vmem_spec(), vmem_spec()),
        compiler_params=limits(8),
        cost_estimate=cost(10 * keep.size, 10 * MIB),
        name="residual",
    )(pos, mine, recv, keep, came, gain)


def gelu(x):
    return x * (0.5 * lax.erf(x * 0.7071067811865476) + 0.5)


def up_kernel(n, dims, pieces, block, pos, own, came, *rest):
    refs, (hidden, weight) = rest[:n], rest[n:]
    lay_out(pos, dims, refs, pieces, weight, block)
    tile = 512
    rows, width = own.shape[1:]
    for k, side in enumerate((own, came)):
        left = side[...].reshape(2 * rows, width)
        for j in range(hidden.shape[-1] // tile):
            at = slice(j * tile, (j + 1) * tile)
            value = gelu(dot(left, weight[:, at])).astype(hidden.dtype).reshape(2, rows, tile)
            if k == 0:
                hidden[0, :, :, at] = value
            else:
                hidden[1, 0, :, at] = value[1]
                hidden[1, 1, :, at] = value[0]


def up_layer(pos, dims, own, came, chunks, pieces, block, units):
    _, rows, width = own.shape
    n = len(chunks)
    return pl.pallas_call(
        functools.partial(up_kernel, n, dims, pieces, block),
        out_shape=jax.ShapeDtypeStruct((2, 2, rows, units), own.dtype),
        in_specs=[smem_spec(), vmem_spec(), vmem_spec()] + [vmem_spec()] * n,
        out_specs=vmem_spec(),
        scratch_shapes=[pltpu.VMEM((width, units), own.dtype)],
        compiler_params=limits(12),
        cost_estimate=cost(8 * rows * width * units, 10 * MIB, 4 * rows * units),
        name="up",
    )(pos, own, came, *chunks)


def down_kernel(n, dims, pieces, block, z_first, pos, hidden, *rest):
    refs, (keep, send, weight) = rest[:n], rest[n:]
    lay_out(pos, dims, refs, pieces, weight, block, z_first)
    for k, result in enumerate((keep, send)):
        left = hidden[k].reshape(-1, hidden.shape[-1])
        result[...] = nt_dot(left, weight[...]).astype(result.dtype).reshape(result.shape)


def down_layer(pos, dims, hidden, chunks, pieces, block, z_first, columns):
    _, _, rows, units = hidden.shape
    n = len(chunks)
    out = jax.ShapeDtypeStruct((2, rows, columns), hidden.dtype)
    return pl.pallas_call(
        functools.partial(down_kernel, n, dims, pieces, block, z_first),
        out_shape=(out, out),
        in_specs=[smem_spec(), vmem_spec()] + [vmem_spec()] * n,
        out_specs=(vmem_spec(), vmem_spec()),
        scratch_shapes=[pltpu.VMEM((columns, units), hidden.dtype)],
        compiler_params=limits(8),
        cost_estimate=cost(8 * rows * columns * units, 8 * MIB),
        name="down",
    )(pos, hidden, *chunks)


def output_kernel(n, nz, starts, pos, residual, targets, *rest):
    parts, (encoded, squares) = rest[:n], rest[n:]
    m = pos[POS_M]
    rows = residual.shape[1]
    total = jnp.zeros((), jnp.float32)
    row_ids = m * rows + lax.broadcasted_iota(jnp.int32, (rows, 1), 0)
    for i in range(2):
        s = pos[POS_STEP] if i == 0 else 1 - pos[POS_STEP]
        usable = row_ids < pos[POS_LEN + i]
        sums = jnp.zeros((rows, 1), jnp.float32)
        for j, spots in enumerate(starts):
            keep, came = parts[2 * j], parts[2 * j + 1]
            size = keep.shape[2] // len(spots)
            for b, back in enumerate(spots):
                at = slice(b * size, (b + 1) * size)
                if back is None:
                    place = pl.ds(0, size)
                else:
                    begin = lax.rem(pos[POS_Z] - back + nz, nz) * size
                    place = pl.ds(pl.multiple_of(begin, size), size)
                value = residual[i, :, place] + (
                    keep[i, :, at].astype(jnp.float32) + came[1 - i, :, at].astype(jnp.float32)
                )
                encoded[s, :, place] = value.astype(encoded.dtype)
                misfit = value - targets[s, :, place].astype(jnp.float32)
                sums = sums + jnp.sum(misfit * misfit, axis=-1, keepdims=True)
        total = total + jnp.sum(jnp.where(usable, sums, 0.0))
    squares[...] = jnp.full(squares.shape, total, jnp.float32)


def output_layer(pos, residual, targets, nz, starts, parts):
    return pl.pallas_call(
        functools.partial(output_kernel, len(parts), nz, starts),
        out_shape=(
            jax.ShapeDtypeStruct(residual.shape, targets.dtype),
            jax.ShapeDtypeStruct((8, 128), jnp.float32),
        ),
        in_specs=[smem_spec()] + [vmem_spec()] * (2 + len(parts)),
        out_specs=(vmem_spec(), vmem_spec()),
        compiler_params=limits(8),
        cost_estimate=cost(8 * residual.size, 8 * MIB),
        name="output",
    )(pos, residual, targets, *parts)


def on_device(
    pixels, counts, owner, embed_weight, w_qkv, w_out, w_up, w_down, ln1_gain, ln2_gain, targets
):
    picture = pixels[0]
    devices, cores = lax.axis_size("dp"), lax.axis_size("mp")
    assert cores == 2
    index, m = lax.axis_index("dp"), lax.axis_index("mp")
    dims = ring_dims(devices)
    width = ln1_gain.shape[0]
    columns = width // cores
    lengths, order = counts[0], owner[0]
    length_mine = jnp.where(m == 0, lengths[0], lengths[1])
    length_other = jnp.where(m == 0, lengths[1], lengths[0])
    step_mine = jnp.where(order[0] == m, 0, 1)
    pos = jnp.stack(
        [
            index // (dims[1] * dims[2]),
            index // dims[2] % dims[1],
            index % dims[2],
            m,
            length_mine,
            length_other,
            step_mine,
            jnp.zeros_like(m),
        ]
    ).astype(jnp.int32)
    gain_halves = ln1_gain.reshape(cores, columns)
    gain_one = jnp.where(m == 0, gain_halves, gain_halves[::-1])

    shards = [embed_weight, w_qkv, w_out.T]
    up, down = w_up, w_down.T
    block, block_e = up.shape[0], embed_weight.shape[0]
    bounds = [0, block_e] + [block_e + (i + 1) * block for i in range(4)]
    last = bounds[-1]
    cut, far_cut = last // 2 // TILE * TILE, (last + block_e) // 2 // TILE * TILE
    units = up.shape[1]
    gain_two = ln2_gain.reshape(1, width)

    def picked(chunks, pieces):
        lists = pieces if isinstance(pieces[0], list) else [pieces]
        used = sorted({p[0] for some in lists for p in some})
        moved = [[(used.index(p[0]), *p[1:]) for p in some] for some in lists]
        return [chunks[i].array for i in used], moved if isinstance(pieces[0], list) else moved[0]

    if dims == (4, 2, 2) and block % (2 * TILE) == 0 and block_e % TILE == 0:
        spans = ((0, cut), (cut, last), (block_e, far_cut), (far_cut, last), (0, block_e), (0, far_cut))
        halves = ((0, block // 2), (block // 2, block))
        work = Gather(*pack_order(pack(shards, up, down), up, down), spans, dims)
        work.slot(0)
        other_picture = swap_columns(picture)
        (other_picture,) = work.end_slot(other_picture)
        for number in range(1, 4):
            work.slot(number)
            (other_picture,) = work.end_slot(other_picture)
        chunks, own_pieces = picked(work.early, pieces_of(work.early, spans, (0, block_e)))
        work.slot(4)
        mine = embed(pos, dims, picture, other_picture, chunks, own_pieces, block_e, columns)
        del work.early
        (mine,) = work.end_slot(mine)
        pieces = [pieces_of(work.parts, spans, (bounds[i], bounds[i + 1])) for i in range(5)]
        work.slot(5)
        recv = swap_columns(mine)
        chunks, own_pieces = picked(work.parts, pieces[1:4])
        q, k, v = project(pos, dims, mine, recv, gain_one, chunks, own_pieces, block, width)
        mine, recv, q, k, v = work.end_slot(mine, recv, q, k, v)
        work.slot(6)
        chunks, own_pieces = picked(work.parts, pieces[4])
        keep, send = attention(pos, dims, q, k, v, chunks, own_pieces, block, width)
        mine, recv, keep, send = work.end_slot(mine, recv, keep, send)
        work.slot(7)
        came = swap_columns(send)
        residual, normed = residual_and_norm(pos, mine, recv, keep, came, gain_two)
        residual, normed = work.end_slot(residual, normed)
        work.slot(8)
        normed_came = swap_columns(normed)
        up_pieces = pieces_of(work.up_parts, halves, (0, block))
        hidden = up_layer(
            pos, dims, normed, normed_came, [c.array for c in work.up_parts], up_pieces, block, units
        )
        residual, hidden = work.end_slot(residual, hidden)
        work.slot(9)
        finals, starts = [], []

        def down_part(part):
            own_pieces = pieces_of(part, halves, (0, block))
            spots = sorted({p[3][0] for p in own_pieces})
            starts.append(spots)
            size = width // dims[0] * len(spots)
            kept, sent = down_layer(
                pos, dims, hidden, [c.array for c in part], own_pieces, block, spots[0], size
            )
            return [kept, sent]

        ready = down_part(work.down_parts[0]) + down_part(work.down_parts[1])
        *ready, residual, hidden = work.end_slot(*ready, residual, hidden)
        finals = [ready[0], swap_columns(ready[1]), ready[2], swap_columns(ready[3])]
        kept, sent = down_part(work.down_parts[2])
        finals += [kept, swap_columns(sent)]
    else:
        *w_three, w_last = [
            lax.all_gather(s, "dp", axis=0, tiled=True)
            for s in (embed_weight, w_qkv[0], w_qkv[1], w_qkv[2], w_out.T, up, down)
        ]
        one = lambda w: [(0, 0, w.shape[0], None, 0)]
        mine = embed(
            pos, dims, picture, swap_columns(picture), w_three[:1], one(w_three[0]), block_e, columns
        )
        recv = swap_columns(mine)
        some = [[(i, 0, w.shape[0], None, 0)] for i, w in enumerate(w_three[1:4])]
        q, k, v = project(pos, dims, mine, recv, gain_one, w_three[1:4], some, block, width)
        keep, send = attention(pos, dims, q, k, v, [w_three[4]], one(w_three[4]), block, width)
        came = swap_columns(send)
        residual, normed = residual_and_norm(pos, mine, recv, keep, came, gain_two)
        hidden = up_layer(
            pos, dims, normed, swap_columns(normed), [w_three[5]], one(w_three[5]), block, units
        )
        kept, sent = down_layer(pos, dims, hidden, [w_last], one(w_last), block, None, width)
        finals, starts = [kept, swap_columns(sent)], [[None]]
    encoded, squares = output_layer(pos, residual, targets[0], dims[0], starts, finals)
    number = jnp.sum(lengths).astype(jnp.float32) / cores
    mine_sums = jnp.stack([squares[0, 0], number])
    sums = lax.all_to_all(
        jnp.broadcast_to(mine_sums[None, None, :], (devices * cores, 1, 2)), ("dp", "mp"), 0, 0, tiled=True
    )
    total_squares, total_number = jnp.sum(sums, axis=(0, 1))
    return (encoded[None], total_squares / (width * total_number))


def solution(mesh):
    in_specs = (
        P(("dp", "mp"), None, None),
        P("dp", None),
        P("dp", None),
        P("dp", "mp"),
        P(None, "dp", "mp"),
        P("mp", "dp"),
        P("dp", "mp"),
        P("mp", "dp"),
        P(),
        P(),
        P("dp", None, "mp", None),
    )
    out_specs = (P("dp", None, "mp", None), P())
    return jax.shard_map(
        on_device, mesh=mesh, in_specs=in_specs, out_specs=out_specs, check_vma=False
    )
```

```python
import functools

import jax
import jax.numpy as jnp
from jax import lax
from jax.experimental import pallas as pl
from jax.experimental.pallas import tpu as pltpu
from jax.sharding import PartitionSpec as P

HEAD = 64
TILE = 16
SPARE = 8
Z, Y, X = 0, 1, 2
MIB = 1 << 20
POS_Z, POS_Y, POS_X, POS_M, POS_LEN, POS_STEP = 0, 1, 2, 3, 4, 6


def ring_dims(count):
    nz = 4 if count % 4 == 0 else 1
    nx = 1
    while nx * nx < count // nz:
        nx *= 2
    ny = count // nz // nx
    return (nz, ny, nx) if nz * ny * nx == count else (1, 1, count)


def shift(value, dims, *axes):
    pairs = []
    for z in range(dims[0]):
        for y in range(dims[1]):
            for x in range(dims[2]):
                to = [z, y, x]
                for axis in axes:
                    to[axis] = (to[axis] + 1) % dims[axis]
                pairs.append(
                    ((z * dims[1] + y) * dims[2] + x, (to[0] * dims[1] + to[1]) * dims[2] + to[2])
                )
    return lax.ppermute(value, "dp", pairs)


class Chunk:
    def __init__(self, array, slots, half, rows, base=0):
        self.array, self.slots, self.half, self.rows, self.base = array, slots, half, rows, base

    def moved(self, array, axis):
        slots = [tuple(v + (i == axis) for i, v in enumerate(s)) for s in self.slots]
        return Chunk(array, slots, self.half, self.rows, self.base)

    def block(self, i, first=0, last=None):
        last = self.rows if last is None else last
        return (self.array, self.base + i * self.rows + first, last - first)

    def all(self, first=0, last=None):
        return [self.block(i, first, last) for i in range(len(self.slots))]


def stack_kernel(plan, *refs):
    sources, results = refs[: -len(plan)], refs[-len(plan) :]
    for result, taken in zip(results, plan, strict=True):
        at = 0
        for number, row, rows in taken:
            result[pl.ds(at, rows), :] = sources[number][pl.ds(row, rows), :]
            at += rows


def stack(*results):
    sources = []
    for taken in results:
        for array, _, _ in taken:
            if all(array is not other for other in sources):
                sources.append(array)

    def number(array):
        return next(i for i, other in enumerate(sources) if other is array)

    plan = [[(number(array), row, rows) for array, row, rows in taken] for taken in results]
    return pl.pallas_call(
        functools.partial(stack_kernel, plan),
        out_shape=tuple(
            jax.ShapeDtypeStruct((sum(rows for _, _, rows in taken), taken[0][0].shape[1]), taken[0][0].dtype)
            for taken in results
        ),
        in_specs=[vmem_spec()] * len(sources),
        out_specs=(vmem_spec(),) * len(results),
        compiler_params=limits(8),
        cost_estimate=cost(0, 2 * MIB),
        name="stack",
    )(*sources)


def swap_columns(value):
    return lax.ppermute(value, "mp", [(0, 1), (1, 0)])


class Gather:
    def __init__(self, first, side_a, side_b, spans, dims):
        self.dims, self.spans, self.half = dims, spans, side_a.shape[0] // 2
        self.first, self.side_a, self.side_b = first, side_a, side_b

    def move(self, value, axis):
        return shift(value, self.dims, axis)

    def step(self, chunk, axis):
        return chunk.moved(shift(chunk.array, self.dims, axis), axis)

    def whole(self, k):
        half = self.half
        sides = (self.side_a, self.from_x, self.side_b, self.from_y)
        return [(side, k * half, half) for side in sides] + [(self.side_a, 0, SPARE)] * (SPARE > 0)

    def ends(self, low, kind):
        first, last = self.spans[kind]
        return [(v, first, last - first) for v in self.first_z[low : low + 2]]

    def chunk(self, array, slots, kind):
        return Chunk(array, slots, kind, self.spans[kind][1] - self.spans[kind][0])

    def both(self, a, b):
        return [a, self.step(a, Y), b, self.step(b, X)]

    def last(self, blocks):
        a, b = stack(
            [c.block(i) for c in blocks for i in (0, 1)], [c.block(i) for c in blocks for i in (2, 3)]
        )
        a = Chunk(a, sum((c.slots[:2] for c in blocks), []), 0, self.half)
        b = Chunk(b, sum((c.slots[2:] for c in blocks), []), 1, self.half)
        return self.both(a, b)

    def slot(self, number):
        if number == 0:
            self.first_z = [self.first, self.move(self.first, Z)]
            self.from_x, self.from_y = self.move(self.side_a, X), self.move(self.side_b, Y)
        elif number == 1:
            self.first_z.append(self.move(self.first_z[-1], Z))
            near = [(0, 0, 0), (1, 0, 0)]
            a, b = stack(self.ends(0, 0), self.ends(0, 1))
            self.a, self.b = self.chunk(a, near, 0), self.chunk(b, near, 1)
            self.a_far, self.b_far = self.step(self.a, X), self.step(self.b, Y)
            up, down = stack(self.whole(0), self.whole(1))
            own = [(0, 0, 0), (0, 0, 1), (0, 0, 0), (0, 1, 0)]
            self.up_z, self.down_z = [Chunk(up, own, 0, self.half)], [Chunk(down, own, 0, self.half)]
        elif number == 2:
            self.first_z.append(self.move(self.first_z[-1], Z))
            del self.side_a, self.side_b, self.from_x, self.from_y
            a, b = stack(self.a.all() + self.a_far.all(), self.b.all() + self.b_far.all())
            self.a = self.chunk(a, self.a.slots + self.a_far.slots, 0)
            self.b = self.chunk(b, self.b.slots + self.b_far.slots, 1)
            self.parts = self.both(self.a, self.b)
        elif number == 3:
            self.up_z.append(self.step(self.up_z[-1], Z))
            far = [(2, 0, 0), (3, 0, 0)]
            a, b, own = stack(self.ends(2, 5), self.ends(2, 3) + self.ends(2, 4), self.ends(2, 4))
            self.a, self.b = self.chunk(a, far, 5), self.chunk(b, far, 3)
            self.a_far, self.b_far = self.step(self.a, X), self.step(self.b, Y)
            corner = self.chunk(shift(own, self.dims, X, Y), [(2, 1, 1), (3, 1, 1)], 4)
            own_far = self.chunk(self.b_far.array, [(2, 1, 0), (3, 1, 0)], 4)
            own_far.base = 2 * self.b.rows
            self.early = self.parts[:2] + [self.a, self.a_far, own_far, corner]
        elif number == 4:
            self.up_z.append(self.step(self.up_z[-1], Z))
            first = self.spans[2][0] - self.spans[5][0]
            a, b = stack(self.a.all(first) + self.a_far.all(first), self.b.all() + self.b_far.all())
            self.a = self.chunk(a, self.a.slots + self.a_far.slots, 2)
            self.b = self.chunk(b, self.b.slots + self.b_far.slots, 3)
            self.parts += self.both(self.a, self.b)
        elif number == 5:
            self.up_parts = self.last(self.up_z[:2])
            self.up_z.append(self.step(self.up_z[-1], Z))
        elif number == 6:
            self.up_parts += self.last(self.up_z[2:])
            self.down_z.append(self.step(self.down_z[-1], Z))
        elif number == 7:
            self.down_parts = [self.last(self.down_z[:2])]
            self.down_z.append(self.step(self.down_z[-1], Z))
        elif number == 8:
            self.down_z.append(self.step(self.down_z[-1], Z))
            self.down_parts.append(self.last(self.down_z[2:3]))
        elif number == 9:
            self.down_parts.append(self.last(self.down_z[3:]))

    def end_slot(self, *others):
        chunks, arrays = [], []
        for name, value in vars(self).items():
            for i, v in enumerate(value if isinstance(value, list) else [value]):
                for k, w in enumerate(v if isinstance(v, list) else [v]):
                    if isinstance(w, Chunk):
                        if all(w is not c for c in chunks):
                            chunks.append(w)
                    elif isinstance(w, jax.Array):
                        arrays.append((name, i, w))
        held = []
        for c in chunks:
            if all(c.array is not w for w in held):
                held.append(c.array)
        together = lax.optimization_barrier((tuple(held), tuple(w for _, _, w in arrays), others))
        for c in chunks:
            c.array = together[0][next(i for i, w in enumerate(held) if w is c.array)]
        for (name, i, _), new in zip(arrays, together[1], strict=True):
            if isinstance(vars(self)[name], list):
                vars(self)[name][i] = new
            else:
                setattr(self, name, new)
        return together[2]


def pieces_of(chunks, spans, segment):
    found = []
    for number, chunk in enumerate(chunks):
        first, last = spans[chunk.half]
        low, high = max(first, segment[0]), min(last, segment[1])
        if low < high:
            for i, slot in enumerate(chunk.slots):
                row = chunk.base + i * chunk.rows + low - first
                found.append((number, row, high - low, slot, low - segment[0]))
    return found


def source(pos, slot, dims, z_first=None):
    z, y, x = (lax.rem(pos[i] - slot[i] + dims[i], dims[i]) for i in (0, 1, 2))
    if z_first is not None:
        z = slot[0] - z_first
    return (z * dims[1] + y) * dims[2] + x


def lay_out(pos, dims, refs, pieces, into, block, z_first=None):
    for number, row, rows, slot, offset in pieces:
        to = offset
        if slot is not None:
            to = pl.multiple_of(source(pos, slot, dims, z_first) * block + offset, TILE)
        into[pl.ds(to, rows), :] = refs[number][pl.ds(row, rows), :]


def nt_dot(left, right):
    return lax.dot_general(left, right, (((1,), (1,)), ((), ())), preferred_element_type=jnp.float32)


def dot(left, right):
    return jnp.dot(left, right, preferred_element_type=jnp.float32)


def any_spec():
    return pl.BlockSpec(memory_space=pl.ANY)


def hbm_spec():
    return pl.BlockSpec(memory_space=pltpu.HBM)


def vmem_spec():
    return pl.BlockSpec(memory_space=pltpu.VMEM)


def smem_spec():
    return pl.BlockSpec(memory_space=pltpu.SMEM)


def limits(mib):
    return pltpu.CompilerParams(vmem_limit_bytes=mib * MIB)


def cost(flops, moved, exps=0):
    return pl.CostEstimate(flops=0, bytes_accessed=1024, transcendentals=0)


def pack_kernel(*rest):
    *shards, up, down, first, side_a, side_b, sems = rest
    half = up.shape[0] // 2
    moves, at = [], 0
    for shard in shards:
        for part in [shard] if len(shard.shape) == 2 else [shard.at[i] for i in range(shard.shape[0])]:
            moves.append((part, first.at[pl.ds(at, part.shape[0])]))
            at += part.shape[0]
    for k, shard in enumerate((up, down)):
        moves.append((shard.at[pl.ds(0, half)], side_a.at[pl.ds(k * half, half)]))
        moves.append((shard.at[pl.ds(half, half)], side_b.at[pl.ds(k * half, half)]))
    made = [pltpu.make_async_copy(a, b, sems.at[i]) for i, (a, b) in enumerate(moves)]
    for c in made:
        c.start()
    for c in made:
        c.wait()


def pack(shards, up, down):
    rows = sum(s.size for s in shards) // shards[0].shape[1]
    first = jax.ShapeDtypeStruct((rows, shards[0].shape[1]), up.dtype)
    side = jax.ShapeDtypeStruct(up.shape, up.dtype)
    return pl.pallas_call(
        pack_kernel,
        out_shape=(first, side, side),
        in_specs=[hbm_spec()] * (len(shards) + 2),
        out_specs=(vmem_spec(),) * 3,
        scratch_shapes=[pltpu.SemaphoreType.DMA((rows // shards[0].shape[0] + 4,))],
        compiler_params=limits(60),
        cost_estimate=cost(0, 2 * MIB),
        name="pack",
    )(*shards, up, down)


def embed_kernel(n, dims, pieces, block, pos, mine, other, *rest):
    refs, (tokens, weight) = rest[:n], rest[n:]
    lay_out(pos, dims, refs, pieces, weight, block)
    tokens[0] = dot(mine[...], weight[...]).astype(tokens.dtype)
    tokens[1] = dot(other[...], weight[...]).astype(tokens.dtype)


def embed(pos, dims, mine, other, chunks, pieces, block, columns):
    patches, pixels = mine.shape
    n = len(chunks)
    return pl.pallas_call(
        functools.partial(embed_kernel, n, dims, pieces, block),
        out_shape=jax.ShapeDtypeStruct((2, patches, columns), mine.dtype),
        in_specs=[smem_spec(), vmem_spec(), vmem_spec()] + [vmem_spec()] * n,
        out_specs=vmem_spec(),
        scratch_shapes=[pltpu.VMEM((pixels, columns), mine.dtype)],
        compiler_params=limits(8),
        cost_estimate=cost(4 * patches * pixels * columns, 4 * MIB),
        name="embed",
    )(pos, mine, other, *chunks)


def project_kernel(n, dims, pieces, block, pos, mine, recv, gain, *rest):
    refs = rest[:n]
    q, k, v, weight, normed = rest[n:]
    m = pos[POS_M]
    columns = mine.shape[2]
    width = 2 * columns
    for i in range(2):
        low = mine[i].astype(jnp.float32)
        high = recv[1 - i].astype(jnp.float32)
        average = (
            jnp.sum(low, axis=-1, keepdims=True) + jnp.sum(high, axis=-1, keepdims=True)
        ) / width
        low, high = low - average, high - average
        spread = (
            jnp.sum(low * low, axis=-1, keepdims=True) + jnp.sum(high * high, axis=-1, keepdims=True)
        ) / width
        scale = lax.rsqrt(spread + 1e-06)
        normed[i, 0] = (low * scale * gain[0:1]).astype(normed.dtype)
        normed[i, 1] = (high * scale * gain[1:2]).astype(normed.dtype)
    here = pl.ds(pl.multiple_of(m * columns, columns), columns)
    there = pl.ds(pl.multiple_of((1 - m) * columns, columns), columns)
    for some, result, factor in zip(pieces, (q, k, v), (HEAD**-0.5, 1.0, 1.0), strict=True):
        lay_out(pos, dims, refs, some, weight, block)
        for i in range(2):
            value = dot(normed[i, 0], weight[here, :]) + dot(normed[i, 1], weight[there, :])
            if factor != 1.0:
                value = value * factor
            result[i] = value.astype(result.dtype)


def project(pos, dims, mine, recv, gain, chunks, pieces, block, width):
    _, patches, columns = mine.shape
    n = len(chunks)
    kind = mine.dtype
    out = jax.ShapeDtypeStruct(mine.shape, kind)
    return pl.pallas_call(
        functools.partial(project_kernel, n, dims, pieces, block),
        out_shape=(out, out, out),
        in_specs=[smem_spec(), vmem_spec(), vmem_spec(), vmem_spec()] + [vmem_spec()] * n,
        out_specs=(vmem_spec(),) * 3,
        scratch_shapes=[
            pltpu.VMEM((width, columns), kind),
            pltpu.VMEM((2, 2, patches, columns), kind),
        ],
        compiler_params=limits(11),
        cost_estimate=cost(2 * 2 * patches * width * columns * 3, 8 * MIB),
        name="project",
    )(pos, mine, recv, gain, *chunks)


def attention_kernel(n, dims, pieces, block, pos, q, k, v, *rest):
    refs = rest[:n]
    keep, send, wo, mixed = rest[n:]
    lay_out(pos, dims, refs, pieces, wo, block)
    m = pos[POS_M]
    patches, columns = q.shape[1:]
    rows_own = patches // 2
    pair = 2 * HEAD
    key_ids = lax.broadcasted_iota(jnp.int32, (1, patches), 1)
    lane = lax.broadcasted_iota(jnp.int32, (patches, pair), 1)
    first = lane < HEAD
    for i in range(2):
        masked = jnp.where(key_ids < pos[POS_LEN + i], 0.0, -1e30).astype(jnp.float32)
        for h in range(columns // pair):
            cut = slice(h * pair, (h + 1) * pair)
            q_pair, k_pair, v_pair = q[i, :, cut], k[i, :, cut], v[i, :, cut]
            found = []
            for own in (first, jnp.logical_not(first)):
                scores = nt_dot(q_pair, jnp.where(own, k_pair, jnp.zeros_like(k_pair))) + masked
                expo = jnp.exp(scores - jnp.max(scores, axis=-1, keepdims=True))
                value = dot(
                    expo.astype(v_pair.dtype), jnp.where(own, v_pair, jnp.ones_like(v_pair))
                )
                found.append(value / pltpu.roll(value, HEAD, 1))
            mixed[i, :, cut] = jnp.where(first, found[0], found[1]).astype(mixed.dtype)
    own_rows = pl.ds(pl.multiple_of(m * rows_own, rows_own), rows_own)
    far_rows = pl.ds(pl.multiple_of((1 - m) * rows_own, rows_own), rows_own)
    for i in range(2):
        keep[i] = nt_dot(mixed[i, own_rows, :], wo[...]).astype(keep.dtype)
        send[i] = nt_dot(mixed[i, far_rows, :], wo[...]).astype(send.dtype)


def attention(pos, dims, q, k, v, chunks, pieces, block, width):
    _, patches, columns = q.shape
    n = len(chunks)
    out = jax.ShapeDtypeStruct((2, patches // 2, width), q.dtype)
    return pl.pallas_call(
        functools.partial(attention_kernel, n, dims, pieces, block),
        out_shape=(out, out),
        in_specs=[smem_spec()] + [vmem_spec()] * 3 + [vmem_spec()] * n,
        out_specs=(vmem_spec(), vmem_spec()),
        scratch_shapes=[
            pltpu.VMEM((width, columns), q.dtype),
            pltpu.VMEM(q.shape, q.dtype),
        ],
        compiler_params=limits(10),
        cost_estimate=cost(
            4 * patches * width * columns + 8 * patches * patches * columns,
            8 * MIB,
            2 * patches * patches * columns // HEAD,
        ),
        name="attention",
    )(pos, q, k, v, *chunks)


def residual_kernel(pos, mine, recv, keep, came, gain, residual, normed):
    m = pos[POS_M]
    columns = mine.shape[2]
    rows = keep.shape[1]
    width = 2 * columns
    own_rows = pl.ds(pl.multiple_of(m * rows, rows), rows)
    here = pl.ds(pl.multiple_of(m * columns, columns), columns)
    there = pl.ds(pl.multiple_of((1 - m) * columns, columns), columns)
    for i in range(2):
        parts = []
        for tokens, at in ((mine[i, own_rows, :], here), (recv[1 - i, own_rows, :], there)):
            parts.append(
                tokens.astype(jnp.float32)
                + (keep[i, :, at].astype(jnp.float32) + came[1 - i, :, at].astype(jnp.float32))
            )
            residual[i, :, at] = parts[-1]
        average = sum(jnp.sum(v, axis=-1, keepdims=True) for v in parts) / width
        parts = [v - average for v in parts]
        spread = sum(jnp.sum(v * v, axis=-1, keepdims=True) for v in parts) / width
        scale = lax.rsqrt(spread + 1e-06)
        for v, at in zip(parts, (here, there), strict=True):
            normed[i, :, at] = (v * scale * gain[0:1, at]).astype(normed.dtype)


def residual_and_norm(pos, mine, recv, keep, came, gain):
    return pl.pallas_call(
        residual_kernel,
        out_shape=(
            jax.ShapeDtypeStruct(keep.shape, jnp.float32),
            jax.ShapeDtypeStruct(keep.shape, keep.dtype),
        ),
        in_specs=[smem_spec()] + [vmem_spec()] * 5,
        out_specs=(vmem_spec(), vmem_spec()),
        compiler_params=limits(8),
        cost_estimate=cost(10 * keep.size, 10 * MIB),
        name="residual",
    )(pos, mine, recv, keep, came, gain)


def gelu(x):
    return x * (0.5 * lax.erf(x * 0.7071067811865476) + 0.5)


def up_kernel(n, dims, pieces, block, pos, own, came, *rest):
    refs, (hidden, weight) = rest[:n], rest[n:]
    lay_out(pos, dims, refs, pieces, weight, block)
    tile = 512
    rows, width = own.shape[1:]
    for k, side in enumerate((own, came)):
        left = side[...].reshape(2 * rows, width)
        for j in range(hidden.shape[-1] // tile):
            at = slice(j * tile, (j + 1) * tile)
            value = gelu(dot(left, weight[:, at])).astype(hidden.dtype).reshape(2, rows, tile)
            if k == 0:
                hidden[0, :, :, at] = value
            else:
                hidden[1, 0, :, at] = value[1]
                hidden[1, 1, :, at] = value[0]


def up_layer(pos, dims, own, came, chunks, pieces, block, units):
    _, rows, width = own.shape
    n = len(chunks)
    return pl.pallas_call(
        functools.partial(up_kernel, n, dims, pieces, block),
        out_shape=jax.ShapeDtypeStruct((2, 2, rows, units), own.dtype),
        in_specs=[smem_spec(), vmem_spec(), vmem_spec()] + [vmem_spec()] * n,
        out_specs=vmem_spec(),
        scratch_shapes=[pltpu.VMEM((width, units), own.dtype)],
        compiler_params=limits(12),
        cost_estimate=cost(8 * rows * width * units, 10 * MIB, 4 * rows * units),
        name="up",
    )(pos, own, came, *chunks)


def down_kernel(n, dims, pieces, block, z_first, pos, hidden, *rest):
    refs, (keep, send, weight) = rest[:n], rest[n:]
    lay_out(pos, dims, refs, pieces, weight, block, z_first)
    for k, result in enumerate((keep, send)):
        left = hidden[k].reshape(-1, hidden.shape[-1])
        result[...] = nt_dot(left, weight[...]).astype(result.dtype).reshape(result.shape)


def down_layer(pos, dims, hidden, chunks, pieces, block, z_first, columns):
    _, _, rows, units = hidden.shape
    n = len(chunks)
    out = jax.ShapeDtypeStruct((2, rows, columns), hidden.dtype)
    return pl.pallas_call(
        functools.partial(down_kernel, n, dims, pieces, block, z_first),
        out_shape=(out, out),
        in_specs=[smem_spec(), vmem_spec()] + [vmem_spec()] * n,
        out_specs=(vmem_spec(), vmem_spec()),
        scratch_shapes=[pltpu.VMEM((columns, units), hidden.dtype)],
        compiler_params=limits(8),
        cost_estimate=cost(8 * rows * columns * units, 8 * MIB),
        name="down",
    )(pos, hidden, *chunks)


def output_kernel(n, nz, starts, ending, pos, residual, targets, *rest):
    parts, (encoded, sums) = rest[:n], rest[-2:]
    m = pos[POS_M]
    rows = residual.shape[1]
    total = jnp.zeros((), jnp.float32)
    row_ids = m * rows + lax.broadcasted_iota(jnp.int32, (rows, 1), 0)
    if ending:
        before, total_before = rest[n : n + 2]
        number = (pos[POS_LEN] + pos[POS_LEN + 1]).astype(jnp.float32) * 0.5
        encoded[...] = before[...]
        total = total_before[0, 0]
    for i in range(2):
        s = pos[POS_STEP] if i == 0 else 1 - pos[POS_STEP]
        usable = row_ids < pos[POS_LEN + i]
        found = jnp.zeros((rows, 1), jnp.float32)
        for j, spots in enumerate(starts):
            keep, came = parts[2 * j], parts[2 * j + 1]
            size = keep.shape[2] // len(spots)
            for b, back in enumerate(spots):
                at = slice(b * size, (b + 1) * size)
                if back is None:
                    place = pl.ds(0, size)
                else:
                    begin = lax.rem(pos[POS_Z] - back + nz, nz) * size
                    place = pl.ds(pl.multiple_of(begin, size), size)
                value = residual[i, :, place] + (
                    keep[i, :, at].astype(jnp.float32) + came[1 - i, :, at].astype(jnp.float32)
                )
                encoded[s, :, place] = value.astype(encoded.dtype)
                misfit = value - targets[s, :, place].astype(jnp.float32)
                found = found + jnp.sum(misfit * misfit, axis=-1, keepdims=True)
        total = total + jnp.sum(jnp.where(usable, found, 0.0))
    if ending:
        lane = lax.broadcasted_iota(jnp.int32, sums.shape, 2)
        sums[...] = jnp.where(lane == 0, total, number)
    else:
        sums[...] = jnp.full(sums.shape, total, jnp.float32)


def output_layer(pos, residual, targets, nz, starts, parts, ending=(), devices=0):
    sums = (devices, 1, 2) if ending else (8, 128)
    specs = [vmem_spec(), vmem_spec()] if ending else []
    return pl.pallas_call(
        functools.partial(output_kernel, len(parts), nz, starts, bool(ending)),
        out_shape=(
            jax.ShapeDtypeStruct(residual.shape, targets.dtype),
            jax.ShapeDtypeStruct(sums, jnp.float32),
        ),
        in_specs=[smem_spec()] + [vmem_spec()] * (2 + len(parts)) + specs,
        out_specs=(vmem_spec(), vmem_spec()),
        compiler_params=limits(8),
        cost_estimate=cost(8 * residual.size, 8 * MIB),
        name="output",
    )(pos, residual, targets, *parts, *ending)


def on_device(
    pixels, counts, owner, embed_weight, w_qkv, w_out, w_up, w_down, ln1_gain, ln2_gain, targets
):
    picture = pixels[0]
    devices, cores = lax.axis_size("dp"), lax.axis_size("mp")
    assert cores == 2
    index, m = lax.axis_index("dp"), lax.axis_index("mp")
    dims = ring_dims(devices)
    width = ln1_gain.shape[0]
    columns = width // cores
    lengths, order = counts[0], owner[0]
    length_mine = jnp.where(m == 0, lengths[0], lengths[1])
    length_other = jnp.where(m == 0, lengths[1], lengths[0])
    step_mine = jnp.where(order[0] == m, 0, 1)
    pos = jnp.stack(
        [
            index // (dims[1] * dims[2]),
            index // dims[2] % dims[1],
            index % dims[2],
            m,
            length_mine,
            length_other,
            step_mine,
            jnp.zeros_like(m),
        ]
    ).astype(jnp.int32)
    gain_halves = ln1_gain.reshape(cores, columns)
    gain_one = jnp.where(m == 0, gain_halves, gain_halves[::-1])

    shards = [embed_weight, w_qkv, w_out.T]
    up, down = w_up, w_down.T
    block, block_e = up.shape[0], embed_weight.shape[0]
    bounds = [0, block_e] + [block_e + (i + 1) * block for i in range(4)]
    last = bounds[-1]
    cut, far_cut = last // 2 // TILE * TILE, (last + block_e) // 2 // TILE * TILE
    units = up.shape[1]
    gain_two = ln2_gain.reshape(1, width)

    def picked(chunks, pieces):
        lists = pieces if isinstance(pieces[0], list) else [pieces]
        used = sorted({p[0] for some in lists for p in some})
        moved = [[(used.index(p[0]), *p[1:]) for p in some] for some in lists]
        return [chunks[i].array for i in used], moved if isinstance(pieces[0], list) else moved[0]

    if dims == (4, 2, 2) and block % (2 * TILE) == 0 and block_e % TILE == 0:
        spans = ((0, cut), (cut, last), (block_e, far_cut), (far_cut, last), (0, block_e), (0, far_cut))
        halves = ((0, block // 2), (block // 2, block))
        work = Gather(*pack(shards, up, down), spans, dims)
        work.slot(0)
        other_picture = swap_columns(picture)
        (other_picture,) = work.end_slot(other_picture)
        for number in range(1, 4):
            work.slot(number)
            (other_picture,) = work.end_slot(other_picture)
        chunks, own_pieces = picked(work.early, pieces_of(work.early, spans, (0, block_e)))
        work.slot(4)
        mine = embed(pos, dims, picture, other_picture, chunks, own_pieces, block_e, columns)
        del work.early
        (mine,) = work.end_slot(mine)
        pieces = [pieces_of(work.parts, spans, (bounds[i], bounds[i + 1])) for i in range(5)]
        work.slot(5)
        recv = swap_columns(mine)
        chunks, own_pieces = picked(work.parts, pieces[1:4])
        q, k, v = project(pos, dims, mine, recv, gain_one, chunks, own_pieces, block, width)
        mine, recv, q, k, v = work.end_slot(mine, recv, q, k, v)
        work.slot(6)
        chunks, own_pieces = picked(work.parts, pieces[4])
        keep, send = attention(pos, dims, q, k, v, chunks, own_pieces, block, width)
        mine, recv, keep, send = work.end_slot(mine, recv, keep, send)
        work.slot(7)
        came = swap_columns(send)
        residual, normed = residual_and_norm(pos, mine, recv, keep, came, gain_two)
        residual, normed = work.end_slot(residual, normed)
        work.slot(8)
        normed_came = swap_columns(normed)
        up_pieces = pieces_of(work.up_parts, halves, (0, block))
        hidden = up_layer(
            pos, dims, normed, normed_came, [c.array for c in work.up_parts], up_pieces, block, units
        )
        residual, hidden = work.end_slot(residual, hidden)
        work.slot(9)
        finals, starts = [], []

        def down_part(part):
            own_pieces = pieces_of(part, halves, (0, block))
            spots = sorted({p[3][0] for p in own_pieces})
            starts.append(spots)
            size = width // dims[0] * len(spots)
            kept, sent = down_layer(
                pos, dims, hidden, [c.array for c in part], own_pieces, block, spots[0], size
            )
            return [kept, sent]

        ready = down_part(work.down_parts[0]) + down_part(work.down_parts[1])
        *ready, residual, hidden = work.end_slot(*ready, residual, hidden)
        finals = [ready[0], swap_columns(ready[1]), ready[2], swap_columns(ready[3])]
        kept, sent = down_part(work.down_parts[2])
        last = [kept, swap_columns(sent)]
    else:
        *w_three, w_last = [
            lax.all_gather(s, "dp", axis=0, tiled=True)
            for s in (embed_weight, w_qkv[0], w_qkv[1], w_qkv[2], w_out.T, up, down)
        ]
        one = lambda w: [(0, 0, w.shape[0], None, 0)]
        mine = embed(
            pos, dims, picture, swap_columns(picture), w_three[:1], one(w_three[0]), block_e, columns
        )
        recv = swap_columns(mine)
        some = [[(i, 0, w.shape[0], None, 0)] for i, w in enumerate(w_three[1:4])]
        q, k, v = project(pos, dims, mine, recv, gain_one, w_three[1:4], some, block, width)
        keep, send = attention(pos, dims, q, k, v, [w_three[4]], one(w_three[4]), block, width)
        came = swap_columns(send)
        residual, normed = residual_and_norm(pos, mine, recv, keep, came, gain_two)
        hidden = up_layer(
            pos, dims, normed, swap_columns(normed), [w_three[5]], one(w_three[5]), block, units
        )
        kept, sent = down_layer(pos, dims, hidden, [w_last], one(w_last), block, None, width)
        finals, starts, last = [], [[None]], [kept, swap_columns(sent)]
    wanted = targets[0]
    if finals:
        encoded, squares = output_layer(pos, residual, wanted, dims[0], starts[:-1], finals)
    else:
        encoded, squares = jnp.zeros_like(wanted), jnp.zeros((8, 128), jnp.float32)
    encoded, sums = output_layer(
        pos,
        residual,
        wanted,
        dims[0],
        starts[-1:],
        last,
        (encoded, squares),
        devices * cores,
    )
    sums = lax.all_to_all(sums, ("dp", "mp"), 0, 0, tiled=True)
    total_squares, total_number = jnp.sum(sums, axis=(0, 1))
    return (encoded[None], total_squares / (width * total_number))


def solution(mesh):
    in_specs = (
        P(("dp", "mp"), None, None),
        P("dp", None),
        P("dp", None),
        P("dp", "mp"),
        P(None, "dp", "mp"),
        P("mp", "dp"),
        P("dp", "mp"),
        P("mp", "dp"),
        P(),
        P(),
        P("dp", None, "mp", None),
    )
    out_specs = (P("dp", None, "mp", None), P())
    return jax.shard_map(
        on_device, mesh=mesh, in_specs=in_specs, out_specs=out_specs, check_vma=False
    )
```

```python
import functools

import jax
import jax.numpy as jnp
from jax import lax
from jax.experimental import pallas as pl
from jax.experimental.pallas import tpu as pltpu
from jax.sharding import PartitionSpec as P

HEAD = 64
TILE = 16
SPARE = 8
Z, Y, X = 0, 1, 2
MIB = 1 << 20
POS_Z, POS_Y, POS_X, POS_M, POS_LEN, POS_STEP = 0, 1, 2, 3, 4, 6


def ring_dims(count):
    nz = 4 if count % 4 == 0 else 1
    nx = 1
    while nx * nx < count // nz:
        nx *= 2
    ny = count // nz // nx
    return (nz, ny, nx) if nz * ny * nx == count else (1, 1, count)


def shift(value, dims, *axes):
    pairs = []
    for z in range(dims[0]):
        for y in range(dims[1]):
            for x in range(dims[2]):
                to = [z, y, x]
                for axis in axes:
                    to[axis] = (to[axis] + 1) % dims[axis]
                pairs.append(
                    ((z * dims[1] + y) * dims[2] + x, (to[0] * dims[1] + to[1]) * dims[2] + to[2])
                )
    return lax.ppermute(value, "dp", pairs)


class Chunk:
    def __init__(self, array, slots, half, rows, base=0):
        self.array, self.slots, self.half, self.rows, self.base = array, slots, half, rows, base

    def moved(self, array, axis):
        slots = [tuple(v + (i == axis) for i, v in enumerate(s)) for s in self.slots]
        return Chunk(array, slots, self.half, self.rows, self.base)

    def block(self, i, first=0, last=None):
        last = self.rows if last is None else last
        return (self.array, self.base + i * self.rows + first, last - first)

    def all(self, first=0, last=None):
        return [self.block(i, first, last) for i in range(len(self.slots))]


def stack_kernel(plan, *refs):
    sources, results = refs[: -len(plan)], refs[-len(plan) :]
    for result, taken in zip(results, plan, strict=True):
        at = 0
        for number, row, rows in taken:
            result[pl.ds(at, rows), :] = sources[number][pl.ds(row, rows), :]
            at += rows


def stack(*results):
    sources = []
    for taken in results:
        for array, _, _ in taken:
            if all(array is not other for other in sources):
                sources.append(array)

    def number(array):
        return next(i for i, other in enumerate(sources) if other is array)

    plan = [[(number(array), row, rows) for array, row, rows in taken] for taken in results]
    return pl.pallas_call(
        functools.partial(stack_kernel, plan),
        out_shape=tuple(
            jax.ShapeDtypeStruct((sum(rows for _, _, rows in taken), taken[0][0].shape[1]), taken[0][0].dtype)
            for taken in results
        ),
        in_specs=[vmem_spec()] * len(sources),
        out_specs=(vmem_spec(),) * len(results),
        compiler_params=limits(8),
        cost_estimate=cost(0, 2 * MIB),
        name="stack",
    )(*sources)


def swap_columns(value):
    return lax.ppermute(value, "mp", [(0, 1), (1, 0)])


class Gather:
    def __init__(self, first, side_a, side_b, spans, dims):
        self.dims, self.spans, self.half = dims, spans, side_a.shape[0] // 2
        self.first, self.side_a, self.side_b = first, side_a, side_b

    def move(self, value, axis):
        return shift(value, self.dims, axis)

    def step(self, chunk, axis):
        return chunk.moved(shift(chunk.array, self.dims, axis), axis)

    def ends(self, low, kind):
        first, last = self.spans[kind]
        return [(v, first, last - first) for v in self.first_z[low : low + 2]]

    def chunk(self, array, slots, kind):
        return Chunk(array, slots, kind, self.spans[kind][1] - self.spans[kind][0])

    def both(self, a, b):
        return [a, self.step(a, Y), b, self.step(b, X)]

    def last(self, first, second):
        a, b = stack(sum((c.all() for c in first), []), sum((c.all() for c in second), []))
        a = Chunk(a, sum((c.slots for c in first), []), 0, self.half)
        b = Chunk(b, sum((c.slots for c in second), []), 1, self.half)
        return self.both(a, b)

    def own_halves(self, k):
        rows = (k * self.half, self.half)
        return ([(self.side_a, *rows), (self.from_x, *rows)], [(self.side_b, *rows), (self.from_y, *rows)])

    def pair(self, b, a):
        (value,) = stack(b.all() + a.all() + [a.block(0, 0, SPARE)])
        return value

    def pair_moved(self, value, b, a):
        value = self.move(value, Z)
        b, a = b.moved(value, Z), a.moved(value, Z)
        b.base, a.base = 0, 2 * self.half
        return b, a, value

    def slot(self, number):
        if number == 0:
            self.first_z = [self.first, self.move(self.first, Z)]
            self.from_x, self.from_y = self.move(self.side_a, X), self.move(self.side_b, Y)
        elif number == 1:
            self.first_z.append(self.move(self.first_z[-1], Z))
            near = [(0, 0, 0), (1, 0, 0)]
            a, b = stack(self.ends(0, 0), self.ends(0, 1))
            self.a, self.b = self.chunk(a, near, 0), self.chunk(b, near, 1)
            self.a_far, self.b_far = self.step(self.a, X), self.step(self.b, Y)
            made = stack(*self.own_halves(0), *self.own_halves(1))
            along_x, along_y = [(0, 0, 0), (0, 0, 1)], [(0, 0, 0), (0, 1, 0)]
            self.up_a, self.down_a = ([Chunk(v, along_x, 0, self.half)] for v in made[0::2])
            self.up_b, self.down_b = ([Chunk(v, along_y, 1, self.half)] for v in made[1::2])
        elif number == 2:
            self.first_z.append(self.move(self.first_z[-1], Z))
            del self.side_a, self.side_b, self.from_x, self.from_y
            a, b = stack(self.a.all() + self.a_far.all(), self.b.all() + self.b_far.all())
            self.a = self.chunk(a, self.a.slots + self.a_far.slots, 0)
            self.b = self.chunk(b, self.b.slots + self.b_far.slots, 1)
            self.parts = self.both(self.a, self.b)
            self.up_a.append(self.step(self.up_a[0], Z))
        elif number == 3:
            value = self.pair(self.up_b[0], self.up_a[1])
            b, a, self.z_pair = self.pair_moved(value, self.up_b[0], self.up_a[1])
            self.up_b.append(b)
            self.up_a.append(a)
            far = [(2, 0, 0), (3, 0, 0)]
            a, b, own = stack(self.ends(2, 5), self.ends(2, 3) + self.ends(2, 4), self.ends(2, 4))
            self.a, self.b = self.chunk(a, far, 5), self.chunk(b, far, 3)
            self.a_far, self.b_far = self.step(self.a, X), self.step(self.b, Y)
            corner = self.chunk(shift(own, self.dims, X, Y), [(2, 1, 1), (3, 1, 1)], 4)
            own_far = self.chunk(self.b_far.array, [(2, 1, 0), (3, 1, 0)], 4)
            own_far.base = 2 * self.b.rows
            self.early = self.parts[:2] + [self.a, self.a_far, own_far, corner]
        elif number == 4:
            b, a, self.z_pair = self.pair_moved(self.z_pair, self.up_b[1], self.up_a[2])
            self.up_b.append(b)
            self.up_a.append(a)
            first = self.spans[2][0] - self.spans[5][0]
            a, b = stack(self.a.all(first) + self.a_far.all(first), self.b.all() + self.b_far.all())
            self.a = self.chunk(a, self.a.slots + self.a_far.slots, 2)
            self.b = self.chunk(b, self.b.slots + self.b_far.slots, 3)
            self.parts += self.both(self.a, self.b)
        elif number == 5:
            value = self.pair(self.up_b[2], self.down_a[0])
            b, a, self.z_pair = self.pair_moved(value, self.up_b[2], self.down_a[0])
            self.up_parts = self.last(self.up_a[:2], self.up_b[:2])
            self.up_b.append(b)
            self.down_a.append(a)
        elif number == 6:
            value = self.pair(self.down_b[0], self.down_a[1])
            b, a, self.z_pair = self.pair_moved(value, self.down_b[0], self.down_a[1])
            self.up_parts += self.last(self.up_a[2:], self.up_b[2:])
            self.down_b.append(b)
            self.down_a.append(a)
        elif number == 7:
            b, a, self.z_pair = self.pair_moved(self.z_pair, self.down_b[1], self.down_a[2])
            self.down_parts = [self.last(self.down_a[:2], self.down_b[:2])]
            self.down_b.append(b)
            self.down_a.append(a)
        elif number == 8:
            del self.z_pair
            (value,) = stack(self.down_b[2].all() + [self.down_b[2].block(0, 0, SPARE)])
            self.down_parts.append(self.last(self.down_a[2:3], self.down_b[2:3]))
            b = self.down_b[2].moved(self.move(value, Z), Z)
            b.base = 0
            self.down_b.append(b)
        elif number == 9:
            self.down_parts.append(self.last(self.down_a[3:], self.down_b[3:]))

    def end_slot(self, *others):
        chunks, arrays = [], []
        for name, value in vars(self).items():
            for i, v in enumerate(value if isinstance(value, list) else [value]):
                for k, w in enumerate(v if isinstance(v, list) else [v]):
                    if isinstance(w, Chunk):
                        if all(w is not c for c in chunks):
                            chunks.append(w)
                    elif isinstance(w, jax.Array):
                        arrays.append((name, i, w))
        held = []
        for c in chunks:
            if all(c.array is not w for w in held):
                held.append(c.array)
        together = lax.optimization_barrier((tuple(held), tuple(w for _, _, w in arrays), others))
        for c in chunks:
            c.array = together[0][next(i for i, w in enumerate(held) if w is c.array)]
        for (name, i, _), new in zip(arrays, together[1], strict=True):
            if isinstance(vars(self)[name], list):
                vars(self)[name][i] = new
            else:
                setattr(self, name, new)
        return together[2]


def pieces_of(chunks, spans, segment):
    found = []
    for number, chunk in enumerate(chunks):
        first, last = spans[chunk.half]
        low, high = max(first, segment[0]), min(last, segment[1])
        if low < high:
            for i, slot in enumerate(chunk.slots):
                row = chunk.base + i * chunk.rows + low - first
                found.append((number, row, high - low, slot, low - segment[0]))
    return found


def wide_pieces(chunks, half, width):
    found = []
    for number, chunk in enumerate(chunks):
        for i, slot in enumerate(chunk.slots):
            for c in range(chunk.rows // half):
                row = chunk.base + i * chunk.rows + c * half
                found.append((number, row, half, slot, chunk.half * half, c * width))
    return found


def source(pos, slot, dims, z_first=None):
    z, y, x = (lax.rem(pos[i] - slot[i] + dims[i], dims[i]) for i in (0, 1, 2))
    if z_first is not None:
        z = slot[0] - z_first
    return (z * dims[1] + y) * dims[2] + x


def lay_out(pos, dims, refs, pieces, into, block, z_first=None):
    for number, row, rows, slot, offset, *column in pieces:
        to = offset
        if slot is not None:
            to = pl.multiple_of(source(pos, slot, dims, z_first) * block + offset, TILE)
        first, width = (column[0] if column else 0), refs[number].shape[1]
        into[pl.ds(to, rows), first : first + width] = refs[number][pl.ds(row, rows), :]


def nt_dot(left, right):
    return lax.dot_general(left, right, (((1,), (1,)), ((), ())), preferred_element_type=jnp.float32)


def dot(left, right):
    return jnp.dot(left, right, preferred_element_type=jnp.float32)


def any_spec():
    return pl.BlockSpec(memory_space=pl.ANY)


def hbm_spec():
    return pl.BlockSpec(memory_space=pltpu.HBM)


def vmem_spec():
    return pl.BlockSpec(memory_space=pltpu.VMEM)


def smem_spec():
    return pl.BlockSpec(memory_space=pltpu.SMEM)


def limits(mib):
    return pltpu.CompilerParams(vmem_limit_bytes=mib * MIB)


def cost(flops, moved, exps=0):
    return pl.CostEstimate(flops=0, bytes_accessed=1024, transcendentals=0)


def pack_kernel(*rest):
    *shards, up, down, first, side_a, side_b, sems = rest
    half, width = up.shape[0] // 2, first.shape[1]
    wide = up.shape[1] // width
    moves, at = [], 0
    for shard in shards:
        for part in [shard] if len(shard.shape) == 2 else [shard.at[i] for i in range(shard.shape[0])]:
            moves.append((part, first.at[pl.ds(at, part.shape[0])]))
            at += part.shape[0]
    for k, shard in enumerate((up, down)):
        for c in range(wide):
            to, columns = pl.ds((k * wide + c) * half, half), pl.ds(c * width, width)
            moves.append((shard.at[pl.ds(0, half), columns], side_a.at[to]))
            moves.append((shard.at[pl.ds(half, half), columns], side_b.at[to]))
    made = [pltpu.make_async_copy(a, b, sems.at[i]) for i, (a, b) in enumerate(moves)]
    for c in made:
        c.start()
    for c in made:
        c.wait()


def pack(shards, up, down):
    rows = sum(s.size for s in shards) // shards[0].shape[1]
    first = jax.ShapeDtypeStruct((rows, shards[0].shape[1]), up.dtype)
    wide = up.shape[1] // shards[0].shape[1]
    side = jax.ShapeDtypeStruct((up.shape[0] * wide, shards[0].shape[1]), up.dtype)
    return pl.pallas_call(
        pack_kernel,
        out_shape=(first, side, side),
        in_specs=[hbm_spec()] * (len(shards) + 2),
        out_specs=(vmem_spec(),) * 3,
        scratch_shapes=[pltpu.SemaphoreType.DMA((len(shards) + 2 + 4 * wide,))],
        compiler_params=limits(60),
        cost_estimate=cost(0, 2 * MIB),
        name="pack",
    )(*shards, up, down)


def embed_kernel(n, dims, pieces, block, pos, mine, other, *rest):
    refs, (tokens, weight) = rest[:n], rest[n:]
    lay_out(pos, dims, refs, pieces, weight, block)
    tokens[0] = dot(mine[...], weight[...]).astype(tokens.dtype)
    tokens[1] = dot(other[...], weight[...]).astype(tokens.dtype)


def embed(pos, dims, mine, other, chunks, pieces, block, columns):
    patches, pixels = mine.shape
    n = len(chunks)
    return pl.pallas_call(
        functools.partial(embed_kernel, n, dims, pieces, block),
        out_shape=jax.ShapeDtypeStruct((2, patches, columns), mine.dtype),
        in_specs=[smem_spec(), vmem_spec(), vmem_spec()] + [vmem_spec()] * n,
        out_specs=vmem_spec(),
        scratch_shapes=[pltpu.VMEM((pixels, columns), mine.dtype)],
        compiler_params=limits(8),
        cost_estimate=cost(4 * patches * pixels * columns, 4 * MIB),
        name="embed",
    )(pos, mine, other, *chunks)


def project_kernel(n, dims, pieces, block, pos, mine, recv, gain, *rest):
    refs = rest[:n]
    q, k, v, weight, normed = rest[n:]
    m = pos[POS_M]
    columns = mine.shape[2]
    width = 2 * columns
    for i in range(2):
        low = mine[i].astype(jnp.float32)
        high = recv[1 - i].astype(jnp.float32)
        average = (
            jnp.sum(low, axis=-1, keepdims=True) + jnp.sum(high, axis=-1, keepdims=True)
        ) / width
        low, high = low - average, high - average
        spread = (
            jnp.sum(low * low, axis=-1, keepdims=True) + jnp.sum(high * high, axis=-1, keepdims=True)
        ) / width
        scale = lax.rsqrt(spread + 1e-06)
        normed[i, 0] = (low * scale * gain[0:1]).astype(normed.dtype)
        normed[i, 1] = (high * scale * gain[1:2]).astype(normed.dtype)
    here = pl.ds(pl.multiple_of(m * columns, columns), columns)
    there = pl.ds(pl.multiple_of((1 - m) * columns, columns), columns)
    for some, result, factor in zip(pieces, (q, k, v), (HEAD**-0.5, 1.0, 1.0), strict=True):
        lay_out(pos, dims, refs, some, weight, block)
        for i in range(2):
            value = dot(normed[i, 0], weight[here, :]) + dot(normed[i, 1], weight[there, :])
            if factor != 1.0:
                value = value * factor
            result[i] = value.astype(result.dtype)


def project(pos, dims, mine, recv, gain, chunks, pieces, block, width):
    _, patches, columns = mine.shape
    n = len(chunks)
    kind = mine.dtype
    out = jax.ShapeDtypeStruct(mine.shape, kind)
    return pl.pallas_call(
        functools.partial(project_kernel, n, dims, pieces, block),
        out_shape=(out, out, out),
        in_specs=[smem_spec(), vmem_spec(), vmem_spec(), vmem_spec()] + [vmem_spec()] * n,
        out_specs=(vmem_spec(),) * 3,
        scratch_shapes=[
            pltpu.VMEM((width, columns), kind),
            pltpu.VMEM((2, 2, patches, columns), kind),
        ],
        compiler_params=limits(11),
        cost_estimate=cost(2 * 2 * patches * width * columns * 3, 8 * MIB),
        name="project",
    )(pos, mine, recv, gain, *chunks)


def attention_kernel(n, dims, pieces, block, pos, q, k, v, *rest):
    refs = rest[:n]
    keep, send, wo, mixed = rest[n:]
    lay_out(pos, dims, refs, pieces, wo, block)
    m = pos[POS_M]
    patches, columns = q.shape[1:]
    rows_own = patches // 2
    pair = 2 * HEAD
    key_ids = lax.broadcasted_iota(jnp.int32, (1, patches), 1)
    lane = lax.broadcasted_iota(jnp.int32, (patches, pair), 1)
    first = lane < HEAD
    for i in range(2):
        masked = jnp.where(key_ids < pos[POS_LEN + i], 0.0, -1e30).astype(jnp.float32)
        for h in range(columns // pair):
            cut = slice(h * pair, (h + 1) * pair)
            q_pair, k_pair, v_pair = q[i, :, cut], k[i, :, cut], v[i, :, cut]
            found = []
            for own in (first, jnp.logical_not(first)):
                scores = nt_dot(q_pair, jnp.where(own, k_pair, jnp.zeros_like(k_pair))) + masked
                expo = jnp.exp(scores - jnp.max(scores, axis=-1, keepdims=True))
                value = dot(
                    expo.astype(v_pair.dtype), jnp.where(own, v_pair, jnp.ones_like(v_pair))
                )
                found.append(value / pltpu.roll(value, HEAD, 1))
            mixed[i, :, cut] = jnp.where(first, found[0], found[1]).astype(mixed.dtype)
    own_rows = pl.ds(pl.multiple_of(m * rows_own, rows_own), rows_own)
    far_rows = pl.ds(pl.multiple_of((1 - m) * rows_own, rows_own), rows_own)
    for i in range(2):
        keep[i] = nt_dot(mixed[i, own_rows, :], wo[...]).astype(keep.dtype)
        send[i] = nt_dot(mixed[i, far_rows, :], wo[...]).astype(send.dtype)


def attention(pos, dims, q, k, v, chunks, pieces, block, width):
    _, patches, columns = q.shape
    n = len(chunks)
    out = jax.ShapeDtypeStruct((2, patches // 2, width), q.dtype)
    return pl.pallas_call(
        functools.partial(attention_kernel, n, dims, pieces, block),
        out_shape=(out, out),
        in_specs=[smem_spec()] + [vmem_spec()] * 3 + [vmem_spec()] * n,
        out_specs=(vmem_spec(), vmem_spec()),
        scratch_shapes=[
            pltpu.VMEM((width, columns), q.dtype),
            pltpu.VMEM(q.shape, q.dtype),
        ],
        compiler_params=limits(10),
        cost_estimate=cost(
            4 * patches * width * columns + 8 * patches * patches * columns,
            8 * MIB,
            2 * patches * patches * columns // HEAD,
        ),
        name="attention",
    )(pos, q, k, v, *chunks)


def residual_kernel(pos, mine, recv, keep, came, gain, residual, normed):
    m = pos[POS_M]
    columns = mine.shape[2]
    rows = keep.shape[1]
    width = 2 * columns
    own_rows = pl.ds(pl.multiple_of(m * rows, rows), rows)
    here = pl.ds(pl.multiple_of(m * columns, columns), columns)
    there = pl.ds(pl.multiple_of((1 - m) * columns, columns), columns)
    for i in range(2):
        parts = []
        for tokens, at in ((mine[i, own_rows, :], here), (recv[1 - i, own_rows, :], there)):
            parts.append(
                tokens.astype(jnp.float32)
                + (keep[i, :, at].astype(jnp.float32) + came[1 - i, :, at].astype(jnp.float32))
            )
            residual[i, :, at] = parts[-1]
        average = sum(jnp.sum(v, axis=-1, keepdims=True) for v in parts) / width
        parts = [v - average for v in parts]
        spread = sum(jnp.sum(v * v, axis=-1, keepdims=True) for v in parts) / width
        scale = lax.rsqrt(spread + 1e-06)
        for v, at in zip(parts, (here, there), strict=True):
            normed[i, :, at] = (v * scale * gain[0:1, at]).astype(normed.dtype)


def residual_and_norm(pos, mine, recv, keep, came, gain):
    return pl.pallas_call(
        residual_kernel,
        out_shape=(
            jax.ShapeDtypeStruct(keep.shape, jnp.float32),
            jax.ShapeDtypeStruct(keep.shape, keep.dtype),
        ),
        in_specs=[smem_spec()] + [vmem_spec()] * 5,
        out_specs=(vmem_spec(), vmem_spec()),
        compiler_params=limits(8),
        cost_estimate=cost(10 * keep.size, 10 * MIB),
        name="residual",
    )(pos, mine, recv, keep, came, gain)


def gelu(x):
    return x * (0.5 * lax.erf(x * 0.7071067811865476) + 0.5)


def up_kernel(n, dims, pieces, block, pos, own, came, *rest):
    refs, (hidden, weight) = rest[:n], rest[n:]
    lay_out(pos, dims, refs, pieces, weight, block)
    tile = 512
    rows, width = own.shape[1:]
    for k, side in enumerate((own, came)):
        left = side[...].reshape(2 * rows, width)
        for j in range(hidden.shape[-1] // tile):
            at = slice(j * tile, (j + 1) * tile)
            value = gelu(dot(left, weight[:, at])).astype(hidden.dtype).reshape(2, rows, tile)
            if k == 0:
                hidden[0, :, :, at] = value
            else:
                hidden[1, 0, :, at] = value[1]
                hidden[1, 1, :, at] = value[0]


def up_layer(pos, dims, own, came, chunks, pieces, block, units):
    _, rows, width = own.shape
    n = len(chunks)
    return pl.pallas_call(
        functools.partial(up_kernel, n, dims, pieces, block),
        out_shape=jax.ShapeDtypeStruct((2, 2, rows, units), own.dtype),
        in_specs=[smem_spec(), vmem_spec(), vmem_spec()] + [vmem_spec()] * n,
        out_specs=vmem_spec(),
        scratch_shapes=[pltpu.VMEM((width, units), own.dtype)],
        compiler_params=limits(12),
        cost_estimate=cost(8 * rows * width * units, 10 * MIB, 4 * rows * units),
        name="up",
    )(pos, own, came, *chunks)


def down_kernel(n, dims, pieces, block, z_first, pos, hidden, *rest):
    refs, (keep, send, weight) = rest[:n], rest[n:]
    lay_out(pos, dims, refs, pieces, weight, block, z_first)
    for k, result in enumerate((keep, send)):
        left = hidden[k].reshape(-1, hidden.shape[-1])
        result[...] = nt_dot(left, weight[...]).astype(result.dtype).reshape(result.shape)


def down_layer(pos, dims, hidden, chunks, pieces, block, z_first, columns):
    _, _, rows, units = hidden.shape
    n = len(chunks)
    out = jax.ShapeDtypeStruct((2, rows, columns), hidden.dtype)
    return pl.pallas_call(
        functools.partial(down_kernel, n, dims, pieces, block, z_first),
        out_shape=(out, out),
        in_specs=[smem_spec(), vmem_spec()] + [vmem_spec()] * n,
        out_specs=(vmem_spec(), vmem_spec()),
        scratch_shapes=[pltpu.VMEM((columns, units), hidden.dtype)],
        compiler_params=limits(8),
        cost_estimate=cost(8 * rows * columns * units, 8 * MIB),
        name="down",
    )(pos, hidden, *chunks)


def output_kernel(n, nz, starts, ending, pos, residual, targets, *rest):
    parts, (encoded, sums) = rest[:n], rest[-2:]
    m = pos[POS_M]
    rows = residual.shape[1]
    total = jnp.zeros((), jnp.float32)
    row_ids = m * rows + lax.broadcasted_iota(jnp.int32, (rows, 1), 0)
    if ending:
        before, total_before = rest[n : n + 2]
        number = (pos[POS_LEN] + pos[POS_LEN + 1]).astype(jnp.float32) * 0.5
        encoded[...] = before[...]
        total = total_before[0, 0]
    for i in range(2):
        s = pos[POS_STEP] if i == 0 else 1 - pos[POS_STEP]
        usable = row_ids < pos[POS_LEN + i]
        found = jnp.zeros((rows, 1), jnp.float32)
        for j, spots in enumerate(starts):
            keep, came = parts[2 * j], parts[2 * j + 1]
            size = keep.shape[2] // len(spots)
            for b, back in enumerate(spots):
                at = slice(b * size, (b + 1) * size)
                if back is None:
                    place = pl.ds(0, size)
                else:
                    begin = lax.rem(pos[POS_Z] - back + nz, nz) * size
                    place = pl.ds(pl.multiple_of(begin, size), size)
                value = residual[i, :, place] + (
                    keep[i, :, at].astype(jnp.float32) + came[1 - i, :, at].astype(jnp.float32)
                )
                encoded[s, :, place] = value.astype(encoded.dtype)
                misfit = value - targets[s, :, place].astype(jnp.float32)
                found = found + jnp.sum(misfit * misfit, axis=-1, keepdims=True)
        total = total + jnp.sum(jnp.where(usable, found, 0.0))
    if ending:
        lane = lax.broadcasted_iota(jnp.int32, sums.shape, 2)
        sums[...] = jnp.where(lane == 0, total, number)
    else:
        sums[...] = jnp.full(sums.shape, total, jnp.float32)


def output_layer(pos, residual, targets, nz, starts, parts, ending=(), devices=0):
    sums = (devices, 1, 2) if ending else (8, 128)
    specs = [vmem_spec(), vmem_spec()] if ending else []
    return pl.pallas_call(
        functools.partial(output_kernel, len(parts), nz, starts, bool(ending)),
        out_shape=(
            jax.ShapeDtypeStruct(residual.shape, targets.dtype),
            jax.ShapeDtypeStruct(sums, jnp.float32),
        ),
        in_specs=[smem_spec()] + [vmem_spec()] * (2 + len(parts)) + specs,
        out_specs=(vmem_spec(), vmem_spec()),
        compiler_params=limits(8),
        cost_estimate=cost(8 * residual.size, 8 * MIB),
        name="output",
    )(pos, residual, targets, *parts, *ending)


def on_device(
    pixels, counts, owner, embed_weight, w_qkv, w_out, w_up, w_down, ln1_gain, ln2_gain, targets
):
    picture = pixels[0]
    devices, cores = lax.axis_size("dp"), lax.axis_size("mp")
    assert cores == 2
    index, m = lax.axis_index("dp"), lax.axis_index("mp")
    dims = ring_dims(devices)
    width = ln1_gain.shape[0]
    columns = width // cores
    lengths, order = counts[0], owner[0]
    length_mine = jnp.where(m == 0, lengths[0], lengths[1])
    length_other = jnp.where(m == 0, lengths[1], lengths[0])
    step_mine = jnp.where(order[0] == m, 0, 1)
    pos = jnp.stack(
        [
            index // (dims[1] * dims[2]),
            index // dims[2] % dims[1],
            index % dims[2],
            m,
            length_mine,
            length_other,
            step_mine,
            jnp.zeros_like(m),
        ]
    ).astype(jnp.int32)
    gain_halves = ln1_gain.reshape(cores, columns)
    gain_one = jnp.where(m == 0, gain_halves, gain_halves[::-1])

    shards = [embed_weight, w_qkv, w_out.T]
    up, down = w_up, w_down.T
    block, block_e = up.shape[0], embed_weight.shape[0]
    bounds = [0, block_e] + [block_e + (i + 1) * block for i in range(4)]
    last = bounds[-1]
    cut, far_cut = last // 2 // TILE * TILE, (last + block_e) // 2 // TILE * TILE
    units = up.shape[1]
    gain_two = ln2_gain.reshape(1, width)

    def picked(chunks, pieces):
        lists = pieces if isinstance(pieces[0], list) else [pieces]
        used = sorted({p[0] for some in lists for p in some})
        moved = [[(used.index(p[0]), *p[1:]) for p in some] for some in lists]
        return [chunks[i].array for i in used], moved if isinstance(pieces[0], list) else moved[0]

    if dims == (4, 2, 2) and block % (2 * TILE) == 0 and block_e % TILE == 0 and units % columns == 0:
        spans = ((0, cut), (cut, last), (block_e, far_cut), (far_cut, last), (0, block_e), (0, far_cut))
        work = Gather(*pack(shards, up, down), spans, dims)
        work.slot(0)
        picture, pos, gain_one = work.end_slot(picture, pos, gain_one)
        work.slot(1)
        picture, pos, gain_one = work.end_slot(picture, pos, gain_one)
        work.slot(2)
        other_picture = swap_columns(picture)
        other_picture, picture = work.end_slot(other_picture, picture)
        work.slot(3)
        other_picture, picture = work.end_slot(other_picture, picture)
        chunks, own_pieces = picked(work.early, pieces_of(work.early, spans, (0, block_e)))
        work.slot(4)
        mine = embed(pos, dims, picture, other_picture, chunks, own_pieces, block_e, columns)
        del work.early
        (mine,) = work.end_slot(mine)
        pieces = [pieces_of(work.parts, spans, (bounds[i], bounds[i + 1])) for i in range(5)]
        work.slot(5)
        recv = swap_columns(mine)
        chunks, own_pieces = picked(work.parts, pieces[1:4])
        q, k, v = project(pos, dims, mine, recv, gain_one, chunks, own_pieces, block, width)
        mine, recv, q, k, v = work.end_slot(mine, recv, q, k, v)
        work.slot(6)
        chunks, own_pieces = picked(work.parts, pieces[4])
        keep, send = attention(pos, dims, q, k, v, chunks, own_pieces, block, width)
        mine, recv, keep, send = work.end_slot(mine, recv, keep, send)
        work.slot(7)
        came = swap_columns(send)
        residual, normed = residual_and_norm(pos, mine, recv, keep, came, gain_two)
        residual, normed = work.end_slot(residual, normed)
        work.slot(8)
        normed_came = swap_columns(normed)
        up_pieces = wide_pieces(work.up_parts, block // 2, columns)
        hidden = up_layer(
            pos, dims, normed, normed_came, [c.array for c in work.up_parts], up_pieces, block, units
        )
        residual, hidden = work.end_slot(residual, hidden)
        work.slot(9)
        finals, starts = [], []

        def down_part(part):
            own_pieces = wide_pieces(part, block // 2, columns)
            spots = sorted({p[3][0] for p in own_pieces})
            starts.append(spots)
            size = width // dims[0] * len(spots)
            kept, sent = down_layer(
                pos, dims, hidden, [c.array for c in part], own_pieces, block, spots[0], size
            )
            return [kept, sent]

        ready = down_part(work.down_parts[0]) + down_part(work.down_parts[1])
        *ready, residual, hidden = work.end_slot(*ready, residual, hidden)
        finals = [ready[0], swap_columns(ready[1]), ready[2], swap_columns(ready[3])]
        kept, sent = down_part(work.down_parts[2])
        last = [kept, swap_columns(sent)]
    else:
        *w_three, w_last = [
            lax.all_gather(s, "dp", axis=0, tiled=True)
            for s in (embed_weight, w_qkv[0], w_qkv[1], w_qkv[2], w_out.T, up, down)
        ]
        one = lambda w: [(0, 0, w.shape[0], None, 0)]
        mine = embed(
            pos, dims, picture, swap_columns(picture), w_three[:1], one(w_three[0]), block_e, columns
        )
        recv = swap_columns(mine)
        some = [[(i, 0, w.shape[0], None, 0)] for i, w in enumerate(w_three[1:4])]
        q, k, v = project(pos, dims, mine, recv, gain_one, w_three[1:4], some, block, width)
        keep, send = attention(pos, dims, q, k, v, [w_three[4]], one(w_three[4]), block, width)
        came = swap_columns(send)
        residual, normed = residual_and_norm(pos, mine, recv, keep, came, gain_two)
        hidden = up_layer(
            pos, dims, normed, swap_columns(normed), [w_three[5]], one(w_three[5]), block, units
        )
        kept, sent = down_layer(pos, dims, hidden, [w_last], one(w_last), block, None, width)
        finals, starts, last = [], [[None]], [kept, swap_columns(sent)]
    wanted = targets[0]
    if finals:
        encoded, squares = output_layer(pos, residual, wanted, dims[0], starts[:-1], finals)
    else:
        encoded, squares = jnp.zeros_like(wanted), jnp.zeros((8, 128), jnp.float32)
    encoded, sums = output_layer(
        pos,
        residual,
        wanted,
        dims[0],
        starts[-1:],
        last,
        (encoded, squares),
        devices * cores,
    )
    sums = lax.all_to_all(sums, ("dp", "mp"), 0, 0, tiled=True)
    total_squares, total_number = jnp.sum(sums, axis=(0, 1))
    return (encoded[None], total_squares / (width * total_number))


def solution(mesh):
    in_specs = (
        P(("dp", "mp"), None, None),
        P("dp", None),
        P("dp", None),
        P("dp", "mp"),
        P(None, "dp", "mp"),
        P("mp", "dp"),
        P("dp", "mp"),
        P("mp", "dp"),
        P(),
        P(),
        P("dp", None, "mp", None),
    )
    out_specs = (P("dp", None, "mp", None), P())
    return jax.shard_map(
        on_device, mesh=mesh, in_specs=in_specs, out_specs=out_specs, check_vma=False
    )
```

```python
import functools

import jax
import jax.numpy as jnp
from jax import lax
from jax.experimental import pallas as pl
from jax.experimental.pallas import tpu as pltpu
from jax.sharding import PartitionSpec as P

HEAD = 64
TILE = 16
SPARE = 8
Z, Y, X = 0, 1, 2
MIB = 1 << 20
POS_Z, POS_Y, POS_X, POS_M, POS_LEN, POS_STEP = 0, 1, 2, 3, 4, 6


def ring_dims(count):
    nz = 4 if count % 4 == 0 else 1
    nx = 1
    while nx * nx < count // nz:
        nx *= 2
    ny = count // nz // nx
    return (nz, ny, nx) if nz * ny * nx == count else (1, 1, count)


def shift(value, dims, *axes):
    pairs = []
    for z in range(dims[0]):
        for y in range(dims[1]):
            for x in range(dims[2]):
                to = [z, y, x]
                for axis in axes:
                    to[axis] = (to[axis] + 1) % dims[axis]
                pairs.append(
                    ((z * dims[1] + y) * dims[2] + x, (to[0] * dims[1] + to[1]) * dims[2] + to[2])
                )
    return lax.ppermute(value, "dp", pairs)


class Chunk:
    def __init__(self, array, slots, half, rows, base=0):
        self.array, self.slots, self.half, self.rows, self.base = array, slots, half, rows, base

    def moved(self, array, axis):
        slots = [tuple(v + (i == axis) for i, v in enumerate(s)) for s in self.slots]
        return Chunk(array, slots, self.half, self.rows, self.base)

    def block(self, i, first=0, last=None):
        last = self.rows if last is None else last
        return (self.array, self.base + i * self.rows + first, last - first)

    def all(self, first=0, last=None):
        return [self.block(i, first, last) for i in range(len(self.slots))]


def stack_kernel(plan, *refs):
    sources, results = refs[: -len(plan)], refs[-len(plan) :]
    for result, taken in zip(results, plan, strict=True):
        at = 0
        for number, row, rows in taken:
            result[pl.ds(at, rows), :] = sources[number][pl.ds(row, rows), :]
            at += rows


def stack(*results):
    sources = []
    for taken in results:
        for array, _, _ in taken:
            if all(array is not other for other in sources):
                sources.append(array)

    def number(array):
        return next(i for i, other in enumerate(sources) if other is array)

    plan = [[(number(array), row, rows) for array, row, rows in taken] for taken in results]
    return pl.pallas_call(
        functools.partial(stack_kernel, plan),
        out_shape=tuple(
            jax.ShapeDtypeStruct((sum(rows for _, _, rows in taken), taken[0][0].shape[1]), taken[0][0].dtype)
            for taken in results
        ),
        in_specs=[vmem_spec()] * len(sources),
        out_specs=(vmem_spec(),) * len(results),
        compiler_params=limits(8),
        cost_estimate=cost(0, 2 * MIB),
        name="stack",
    )(*sources)


def swap_columns(value):
    return lax.ppermute(value, "mp", [(0, 1), (1, 0)])


class Gather:
    def __init__(self, first, side_a, side_b, spans, dims):
        self.dims, self.spans, self.half = dims, spans, side_a.shape[0] // 2
        self.first, self.side_a, self.side_b = first, side_a, side_b

    def move(self, value, axis):
        return shift(value, self.dims, axis)

    def step(self, chunk, axis):
        return chunk.moved(shift(chunk.array, self.dims, axis), axis)

    def ends(self, low, kind):
        first, last = self.spans[kind]
        return [(v, first, last - first) for v in self.first_z[low : low + 2]]

    def chunk(self, array, slots, kind):
        return Chunk(array, slots, kind, self.spans[kind][1] - self.spans[kind][0])

    def both(self, a, b):
        return [a, self.step(a, Y), b, self.step(b, X)]

    def last(self, first, second):
        a, b = stack(sum((c.all() for c in first), []), sum((c.all() for c in second), []))
        a = Chunk(a, sum((c.slots for c in first), []), 0, self.half)
        b = Chunk(b, sum((c.slots for c in second), []), 1, self.half)
        return self.both(a, b)

    def own_halves(self, k):
        rows = (k * self.half, self.half)
        return ([(self.side_a, *rows), (self.from_x, *rows)], [(self.side_b, *rows), (self.from_y, *rows)])

    def pair(self, b, a):
        (value,) = stack(b.all() + a.all() + [a.block(0, 0, SPARE)])
        return value

    def pair_moved(self, value, b, a):
        value = self.move(value, Z)
        b, a = b.moved(value, Z), a.moved(value, Z)
        b.base, a.base = 0, 2 * self.half
        return b, a, value

    def slot(self, number):
        if number == 0:
            self.first_z = [self.first, self.move(self.first, Z)]
            self.from_x, self.from_y = self.move(self.side_a, X), self.move(self.side_b, Y)
        elif number == 1:
            self.first_z.append(self.move(self.first_z[-1], Z))
            near = [(0, 0, 0), (1, 0, 0)]
            a, *b = stack(self.ends(0, 0), self.ends(0, 1)[:1], self.ends(0, 1)[1:])
            self.a = self.chunk(a, near, 0)
            self.b = [self.chunk(v, near[i : i + 1], 1) for i, v in enumerate(b)]
            self.a_far, self.b_far = self.step(self.a, X), [self.step(c, Y) for c in self.b]
            made = stack(*self.own_halves(0), *self.own_halves(1))
            along_x, along_y = [(0, 0, 0), (0, 0, 1)], [(0, 0, 0), (0, 1, 0)]
            self.up_a, self.down_a = ([Chunk(v, along_x, 0, self.half)] for v in made[0::2])
            self.up_b, self.down_b = ([Chunk(v, along_y, 1, self.half)] for v in made[1::2])
        elif number == 2:
            self.first_z.append(self.move(self.first_z[-1], Z))
            del self.side_a, self.side_b, self.from_x, self.from_y
            from_b = self.b + self.b_far
            a, b = stack(self.a.all() + self.a_far.all(), sum((c.all() for c in from_b), []))
            self.a = self.chunk(a, self.a.slots + self.a_far.slots, 0)
            self.b = self.chunk(b, sum((c.slots for c in from_b), []), 1)
            self.parts = self.both(self.a, self.b)
            self.up_a.append(self.step(self.up_a[0], Z))
        elif number == 3:
            value = self.pair(self.up_b[0], self.up_a[1])
            b, a, self.z_pair = self.pair_moved(value, self.up_b[0], self.up_a[1])
            self.up_b.append(b)
            self.up_a.append(a)
            far = [(2, 0, 0), (3, 0, 0)]
            a, b, own = stack(self.ends(2, 5), self.ends(2, 3) + self.ends(2, 4), self.ends(2, 4))
            self.a, self.b = self.chunk(a, far, 5), self.chunk(b, far, 3)
            self.a_far, self.b_far = self.step(self.a, X), self.step(self.b, Y)
            corner = self.chunk(shift(own, self.dims, X, Y), [(2, 1, 1), (3, 1, 1)], 4)
            own_far = self.chunk(self.b_far.array, [(2, 1, 0), (3, 1, 0)], 4)
            own_far.base = 2 * self.b.rows
            self.early = self.parts[:2] + [self.a, self.a_far, own_far, corner]
        elif number == 4:
            b, a, self.z_pair = self.pair_moved(self.z_pair, self.up_b[1], self.up_a[2])
            self.up_b.append(b)
            self.up_a.append(a)
            first = self.spans[2][0] - self.spans[5][0]
            a, b = stack(self.a.all(first) + self.a_far.all(first), self.b.all() + self.b_far.all())
            self.a = self.chunk(a, self.a.slots + self.a_far.slots, 2)
            self.b = self.chunk(b, self.b.slots + self.b_far.slots, 3)
            self.parts += self.both(self.a, self.b)
        elif number == 5:
            value = self.pair(self.up_b[2], self.down_a[0])
            b, a, self.z_pair = self.pair_moved(value, self.up_b[2], self.down_a[0])
            self.up_parts = self.last(self.up_a[:2], self.up_b[:2])
            self.up_b.append(b)
            self.down_a.append(a)
        elif number == 6:
            value = self.pair(self.down_b[0], self.down_a[1])
            b, a, self.z_pair = self.pair_moved(value, self.down_b[0], self.down_a[1])
            self.up_parts += self.last(self.up_a[2:], self.up_b[2:])
            self.down_b.append(b)
            self.down_a.append(a)
        elif number == 7:
            b, a, self.z_pair = self.pair_moved(self.z_pair, self.down_b[1], self.down_a[2])
            self.down_parts = [self.last(self.down_a[:2], self.down_b[:2])]
            self.down_b.append(b)
            self.down_a.append(a)
        elif number == 8:
            del self.z_pair
            far_a, far_b = self.down_a[2:], self.down_b[2]
            value, near = stack(*(c.all() + [c.block(0, 0, SPARE)] for c in (far_b, far_a[0])))
            ahead, near = Chunk(value, far_b.slots, 1, self.half), Chunk(near, far_a[0].slots, 0, self.half)
            corner = ahead.moved(shift(value, self.dims, Z, X), Z)
            corner = corner.moved(corner.array, X)
            near_far = self.step(near, Y)
            b, a = stack(far_b.all(), far_a[1].all())
            b, a = Chunk(b, far_b.slots, 1, self.half), Chunk(a, far_a[1].slots, 0, self.half)
            self.down_parts.append(
                [near, near_far, b, self.step(b, X), a, self.step(a, Y), self.step(b, Z), corner]
            )

    def end_slot(self, *others):
        chunks, arrays = [], []
        for name, value in vars(self).items():
            for i, v in enumerate(value if isinstance(value, list) else [value]):
                for k, w in enumerate(v if isinstance(v, list) else [v]):
                    if isinstance(w, Chunk):
                        if all(w is not c for c in chunks):
                            chunks.append(w)
                    elif isinstance(w, jax.Array):
                        arrays.append((name, i, w))
        held = []
        for c in chunks:
            if all(c.array is not w for w in held):
                held.append(c.array)
        together = lax.optimization_barrier((tuple(held), tuple(w for _, _, w in arrays), others))
        for c in chunks:
            c.array = together[0][next(i for i, w in enumerate(held) if w is c.array)]
        for (name, i, _), new in zip(arrays, together[1], strict=True):
            if isinstance(vars(self)[name], list):
                vars(self)[name][i] = new
            else:
                setattr(self, name, new)
        return together[2]


def pieces_of(chunks, spans, segment):
    found = []
    for number, chunk in enumerate(chunks):
        first, last = spans[chunk.half]
        low, high = max(first, segment[0]), min(last, segment[1])
        if low < high:
            for i, slot in enumerate(chunk.slots):
                row = chunk.base + i * chunk.rows + low - first
                found.append((number, row, high - low, slot, low - segment[0]))
    return found


def wide_pieces(chunks, half, width):
    found = []
    for number, chunk in enumerate(chunks):
        for i, slot in enumerate(chunk.slots):
            for c in range(chunk.rows // half):
                row = chunk.base + i * chunk.rows + c * half
                found.append((number, row, half, slot, chunk.half * half, c * width))
    return found


def source(pos, slot, dims, z_first=None):
    z, y, x = (lax.rem(pos[i] - slot[i] + dims[i], dims[i]) for i in (0, 1, 2))
    if z_first is not None:
        z = slot[0] - z_first
    return (z * dims[1] + y) * dims[2] + x


def lay_out(pos, dims, refs, pieces, into, block, z_first=None):
    for number, row, rows, slot, offset, *column in pieces:
        to = offset
        if slot is not None:
            to = pl.multiple_of(source(pos, slot, dims, z_first) * block + offset, TILE)
        first, width = (column[0] if column else 0), refs[number].shape[1]
        into[pl.ds(to, rows), first : first + width] = refs[number][pl.ds(row, rows), :]


def nt_dot(left, right):
    return lax.dot_general(left, right, (((1,), (1,)), ((), ())), preferred_element_type=jnp.float32)


def dot(left, right):
    return jnp.dot(left, right, preferred_element_type=jnp.float32)


def any_spec():
    return pl.BlockSpec(memory_space=pl.ANY)


def hbm_spec():
    return pl.BlockSpec(memory_space=pltpu.HBM)


def vmem_spec():
    return pl.BlockSpec(memory_space=pltpu.VMEM)


def smem_spec():
    return pl.BlockSpec(memory_space=pltpu.SMEM)


def limits(mib):
    return pltpu.CompilerParams(vmem_limit_bytes=mib * MIB)


def cost(flops, moved, exps=0):
    return pl.CostEstimate(flops=0, bytes_accessed=1024, transcendentals=0)


def pack_kernel(*rest):
    *shards, up, down, first, side_a, side_b, sems = rest
    half, width = up.shape[0] // 2, first.shape[1]
    wide = up.shape[1] // width
    moves, at = [], 0
    for shard in shards:
        for part in [shard] if len(shard.shape) == 2 else [shard.at[i] for i in range(shard.shape[0])]:
            moves.append((part, first.at[pl.ds(at, part.shape[0])]))
            at += part.shape[0]
    for k, shard in enumerate((up, down)):
        for c in range(wide):
            to, columns = pl.ds((k * wide + c) * half, half), pl.ds(c * width, width)
            moves.append((shard.at[pl.ds(0, half), columns], side_a.at[to]))
            moves.append((shard.at[pl.ds(half, half), columns], side_b.at[to]))
    made = [pltpu.make_async_copy(a, b, sems.at[i]) for i, (a, b) in enumerate(moves)]
    for c in made:
        c.start()
    for c in made:
        c.wait()


def pack(shards, up, down):
    rows = sum(s.size for s in shards) // shards[0].shape[1]
    first = jax.ShapeDtypeStruct((rows, shards[0].shape[1]), up.dtype)
    wide = up.shape[1] // shards[0].shape[1]
    side = jax.ShapeDtypeStruct((up.shape[0] * wide, shards[0].shape[1]), up.dtype)
    return pl.pallas_call(
        pack_kernel,
        out_shape=(first, side, side),
        in_specs=[hbm_spec()] * (len(shards) + 2),
        out_specs=(vmem_spec(),) * 3,
        scratch_shapes=[pltpu.SemaphoreType.DMA((len(shards) + 2 + 4 * wide,))],
        compiler_params=limits(60),
        cost_estimate=cost(0, 2 * MIB),
        name="pack",
    )(*shards, up, down)


def embed_kernel(n, dims, pieces, block, pos, mine, other, *rest):
    refs, (tokens, weight) = rest[:n], rest[n:]
    lay_out(pos, dims, refs, pieces, weight, block)
    tokens[0] = dot(mine[...], weight[...]).astype(tokens.dtype)
    tokens[1] = dot(other[...], weight[...]).astype(tokens.dtype)


def embed(pos, dims, mine, other, chunks, pieces, block, columns):
    patches, pixels = mine.shape
    n = len(chunks)
    return pl.pallas_call(
        functools.partial(embed_kernel, n, dims, pieces, block),
        out_shape=jax.ShapeDtypeStruct((2, patches, columns), mine.dtype),
        in_specs=[smem_spec(), vmem_spec(), vmem_spec()] + [vmem_spec()] * n,
        out_specs=vmem_spec(),
        scratch_shapes=[pltpu.VMEM((pixels, columns), mine.dtype)],
        compiler_params=limits(8),
        cost_estimate=cost(4 * patches * pixels * columns, 4 * MIB),
        name="embed",
    )(pos, mine, other, *chunks)


def project_kernel(n, dims, pieces, block, pos, mine, recv, gain, *rest):
    refs = rest[:n]
    q, k, v, weight, normed = rest[n:]
    m = pos[POS_M]
    columns = mine.shape[2]
    width = 2 * columns
    for i in range(2):
        low = mine[i].astype(jnp.float32)
        high = recv[1 - i].astype(jnp.float32)
        average = (
            jnp.sum(low, axis=-1, keepdims=True) + jnp.sum(high, axis=-1, keepdims=True)
        ) / width
        low, high = low - average, high - average
        spread = (
            jnp.sum(low * low, axis=-1, keepdims=True) + jnp.sum(high * high, axis=-1, keepdims=True)
        ) / width
        scale = lax.rsqrt(spread + 1e-06)
        normed[i, 0] = (low * scale * gain[0:1]).astype(normed.dtype)
        normed[i, 1] = (high * scale * gain[1:2]).astype(normed.dtype)
    here = pl.ds(pl.multiple_of(m * columns, columns), columns)
    there = pl.ds(pl.multiple_of((1 - m) * columns, columns), columns)
    for some, result, factor in zip(pieces, (q, k, v), (HEAD**-0.5, 1.0, 1.0), strict=True):
        lay_out(pos, dims, refs, some, weight, block)
        for i in range(2):
            value = dot(normed[i, 0], weight[here, :]) + dot(normed[i, 1], weight[there, :])
            if factor != 1.0:
                value = value * factor
            result[i] = value.astype(result.dtype)


def project(pos, dims, mine, recv, gain, chunks, pieces, block, width):
    _, patches, columns = mine.shape
    n = len(chunks)
    kind = mine.dtype
    out = jax.ShapeDtypeStruct(mine.shape, kind)
    return pl.pallas_call(
        functools.partial(project_kernel, n, dims, pieces, block),
        out_shape=(out, out, out),
        in_specs=[smem_spec(), vmem_spec(), vmem_spec(), vmem_spec()] + [vmem_spec()] * n,
        out_specs=(vmem_spec(),) * 3,
        scratch_shapes=[
            pltpu.VMEM((width, columns), kind),
            pltpu.VMEM((2, 2, patches, columns), kind),
        ],
        compiler_params=limits(11),
        cost_estimate=cost(2 * 2 * patches * width * columns * 3, 8 * MIB),
        name="project",
    )(pos, mine, recv, gain, *chunks)


def attention_kernel(n, dims, pieces, block, pos, q, k, v, *rest):
    refs = rest[:n]
    keep, send, wo, mixed = rest[n:]
    lay_out(pos, dims, refs, pieces, wo, block)
    m = pos[POS_M]
    patches, columns = q.shape[1:]
    rows_own = patches // 2
    pair = 2 * HEAD
    key_ids = lax.broadcasted_iota(jnp.int32, (1, patches), 1)
    lane = lax.broadcasted_iota(jnp.int32, (patches, pair), 1)
    first = lane < HEAD
    for i in range(2):
        masked = jnp.where(key_ids < pos[POS_LEN + i], 0.0, -1e30).astype(jnp.float32)
        for h in range(columns // pair):
            cut = slice(h * pair, (h + 1) * pair)
            q_pair, k_pair, v_pair = q[i, :, cut], k[i, :, cut], v[i, :, cut]
            found = []
            for own in (first, jnp.logical_not(first)):
                scores = nt_dot(q_pair, jnp.where(own, k_pair, jnp.zeros_like(k_pair))) + masked
                expo = jnp.exp(scores - jnp.max(scores, axis=-1, keepdims=True))
                value = dot(
                    expo.astype(v_pair.dtype), jnp.where(own, v_pair, jnp.ones_like(v_pair))
                )
                found.append(value / pltpu.roll(value, HEAD, 1))
            mixed[i, :, cut] = jnp.where(first, found[0], found[1]).astype(mixed.dtype)
    own_rows = pl.ds(pl.multiple_of(m * rows_own, rows_own), rows_own)
    far_rows = pl.ds(pl.multiple_of((1 - m) * rows_own, rows_own), rows_own)
    for i in range(2):
        keep[i] = nt_dot(mixed[i, own_rows, :], wo[...]).astype(keep.dtype)
        send[i] = nt_dot(mixed[i, far_rows, :], wo[...]).astype(send.dtype)


def attention(pos, dims, q, k, v, chunks, pieces, block, width):
    _, patches, columns = q.shape
    n = len(chunks)
    out = jax.ShapeDtypeStruct((2, patches // 2, width), q.dtype)
    return pl.pallas_call(
        functools.partial(attention_kernel, n, dims, pieces, block),
        out_shape=(out, out),
        in_specs=[smem_spec()] + [vmem_spec()] * 3 + [vmem_spec()] * n,
        out_specs=(vmem_spec(), vmem_spec()),
        scratch_shapes=[
            pltpu.VMEM((width, columns), q.dtype),
            pltpu.VMEM(q.shape, q.dtype),
        ],
        compiler_params=limits(10),
        cost_estimate=cost(
            4 * patches * width * columns + 8 * patches * patches * columns,
            8 * MIB,
            2 * patches * patches * columns // HEAD,
        ),
        name="attention",
    )(pos, q, k, v, *chunks)


def residual_kernel(pos, mine, recv, keep, came, gain, residual, normed):
    m = pos[POS_M]
    columns = mine.shape[2]
    rows = keep.shape[1]
    width = 2 * columns
    own_rows = pl.ds(pl.multiple_of(m * rows, rows), rows)
    here = pl.ds(pl.multiple_of(m * columns, columns), columns)
    there = pl.ds(pl.multiple_of((1 - m) * columns, columns), columns)
    for i in range(2):
        parts = []
        for tokens, at in ((mine[i, own_rows, :], here), (recv[1 - i, own_rows, :], there)):
            parts.append(
                tokens.astype(jnp.float32)
                + (keep[i, :, at].astype(jnp.float32) + came[1 - i, :, at].astype(jnp.float32))
            )
            residual[i, :, at] = parts[-1]
        average = sum(jnp.sum(v, axis=-1, keepdims=True) for v in parts) / width
        parts = [v - average for v in parts]
        spread = sum(jnp.sum(v * v, axis=-1, keepdims=True) for v in parts) / width
        scale = lax.rsqrt(spread + 1e-06)
        for v, at in zip(parts, (here, there), strict=True):
            normed[i, :, at] = (v * scale * gain[0:1, at]).astype(normed.dtype)


def residual_and_norm(pos, mine, recv, keep, came, gain):
    return pl.pallas_call(
        residual_kernel,
        out_shape=(
            jax.ShapeDtypeStruct(keep.shape, jnp.float32),
            jax.ShapeDtypeStruct(keep.shape, keep.dtype),
        ),
        in_specs=[smem_spec()] + [vmem_spec()] * 5,
        out_specs=(vmem_spec(), vmem_spec()),
        compiler_params=limits(8),
        cost_estimate=cost(10 * keep.size, 10 * MIB),
        name="residual",
    )(pos, mine, recv, keep, came, gain)


def gelu(x):
    return x * (0.5 * lax.erf(x * 0.7071067811865476) + 0.5)


def up_kernel(n, dims, pieces, block, pos, own, came, *rest):
    refs, (hidden, weight) = rest[:n], rest[n:]
    lay_out(pos, dims, refs, pieces, weight, block)
    tile = 512
    rows, width = own.shape[1:]
    for k, side in enumerate((own, came)):
        left = side[...].reshape(2 * rows, width)
        for j in range(hidden.shape[-1] // tile):
            at = slice(j * tile, (j + 1) * tile)
            value = gelu(dot(left, weight[:, at])).astype(hidden.dtype).reshape(2, rows, tile)
            if k == 0:
                hidden[0, :, :, at] = value
            else:
                hidden[1, 0, :, at] = value[1]
                hidden[1, 1, :, at] = value[0]


def up_layer(pos, dims, own, came, chunks, pieces, block, units):
    _, rows, width = own.shape
    n = len(chunks)
    return pl.pallas_call(
        functools.partial(up_kernel, n, dims, pieces, block),
        out_shape=jax.ShapeDtypeStruct((2, 2, rows, units), own.dtype),
        in_specs=[smem_spec(), vmem_spec(), vmem_spec()] + [vmem_spec()] * n,
        out_specs=vmem_spec(),
        scratch_shapes=[pltpu.VMEM((width, units), own.dtype)],
        compiler_params=limits(12),
        cost_estimate=cost(8 * rows * width * units, 10 * MIB, 4 * rows * units),
        name="up",
    )(pos, own, came, *chunks)


def down_kernel(n, dims, pieces, block, z_first, pos, hidden, *rest):
    refs, (keep, send, weight) = rest[:n], rest[n:]
    lay_out(pos, dims, refs, pieces, weight, block, z_first)
    for k, result in enumerate((keep, send)):
        left = hidden[k].reshape(-1, hidden.shape[-1])
        result[...] = nt_dot(left, weight[...]).astype(result.dtype).reshape(result.shape)


def down_layer(pos, dims, hidden, chunks, pieces, block, z_first, columns):
    _, _, rows, units = hidden.shape
    n = len(chunks)
    out = jax.ShapeDtypeStruct((2, rows, columns), hidden.dtype)
    return pl.pallas_call(
        functools.partial(down_kernel, n, dims, pieces, block, z_first),
        out_shape=(out, out),
        in_specs=[smem_spec(), vmem_spec()] + [vmem_spec()] * n,
        out_specs=(vmem_spec(), vmem_spec()),
        scratch_shapes=[pltpu.VMEM((columns, units), hidden.dtype)],
        compiler_params=limits(8),
        cost_estimate=cost(8 * rows * columns * units, 8 * MIB),
        name="down",
    )(pos, hidden, *chunks)


def output_kernel(n, nz, starts, ending, pos, residual, targets, *rest):
    parts, (encoded, sums) = rest[:n], rest[-2:]
    m = pos[POS_M]
    rows = residual.shape[1]
    total = jnp.zeros((), jnp.float32)
    row_ids = m * rows + lax.broadcasted_iota(jnp.int32, (rows, 1), 0)
    if ending:
        before, total_before = rest[n : n + 2]
        encoded[...] = before[...]
        number = (pos[POS_LEN] + pos[POS_LEN + 1]).astype(jnp.float32) * 0.5
        total = total_before[0, 0]
    for i in range(2):
        s = pos[POS_STEP] if i == 0 else 1 - pos[POS_STEP]
        usable = row_ids < pos[POS_LEN + i]
        found = jnp.zeros((rows, 1), jnp.float32)
        for j, spots in enumerate(starts):
            keep, came = parts[2 * j], parts[2 * j + 1]
            size = keep.shape[2] // len(spots)
            for b, back in enumerate(spots):
                at = slice(b * size, (b + 1) * size)
                if back is None:
                    place = pl.ds(0, size)
                else:
                    begin = lax.rem(pos[POS_Z] - back + nz, nz) * size
                    place = pl.ds(pl.multiple_of(begin, size), size)
                value = residual[i, :, place] + (
                    keep[i, :, at].astype(jnp.float32) + came[1 - i, :, at].astype(jnp.float32)
                )
                encoded[s, :, place] = value.astype(encoded.dtype)
                misfit = value - targets[s, :, place].astype(jnp.float32)
                found = found + jnp.sum(misfit * misfit, axis=-1, keepdims=True)
        total = total + jnp.sum(jnp.where(usable, found, 0.0))
    if ending:
        lane = lax.broadcasted_iota(jnp.int32, sums.shape, 2)
        sums[...] = jnp.where(lane == 0, total, number)
    else:
        sums[...] = jnp.full(sums.shape, total, jnp.float32)


def output_layer(pos, residual, targets, nz, starts, parts, ending=(), devices=0):
    sums = (devices, 1, 2) if ending else (8, 128)
    specs = [vmem_spec(), vmem_spec()] if ending else []
    return pl.pallas_call(
        functools.partial(output_kernel, len(parts), nz, starts, bool(ending)),
        out_shape=(
            jax.ShapeDtypeStruct(residual.shape, targets.dtype),
            jax.ShapeDtypeStruct(sums, jnp.float32),
        ),
        in_specs=[smem_spec()] + [vmem_spec()] * (2 + len(parts)) + specs,
        out_specs=(vmem_spec(), vmem_spec()),
        compiler_params=limits(8),
        cost_estimate=cost(8 * residual.size, 8 * MIB),
        name="output",
    )(pos, residual, targets, *parts, *ending)


def on_device(
    pixels, counts, owner, embed_weight, w_qkv, w_out, w_up, w_down, ln1_gain, ln2_gain, targets
):
    picture = pixels[0]
    devices, cores = lax.axis_size("dp"), lax.axis_size("mp")
    assert cores == 2
    index, m = lax.axis_index("dp"), lax.axis_index("mp")
    dims = ring_dims(devices)
    width = ln1_gain.shape[0]
    columns = width // cores
    lengths, order = counts[0], owner[0]
    length_mine = jnp.where(m == 0, lengths[0], lengths[1])
    length_other = jnp.where(m == 0, lengths[1], lengths[0])
    step_mine = jnp.where(order[0] == m, 0, 1)
    pos = jnp.stack(
        [
            index // (dims[1] * dims[2]),
            index // dims[2] % dims[1],
            index % dims[2],
            m,
            length_mine,
            length_other,
            step_mine,
            jnp.zeros_like(m),
        ]
    ).astype(jnp.int32)
    gain_halves = ln1_gain.reshape(cores, columns)
    gain_one = jnp.where(m == 0, gain_halves, gain_halves[::-1])

    shards = [embed_weight, w_qkv, w_out.T]
    up, down = w_up, w_down.T
    block, block_e = up.shape[0], embed_weight.shape[0]
    bounds = [0, block_e] + [block_e + (i + 1) * block for i in range(4)]
    last = bounds[-1]
    cut, far_cut = last // 2 // TILE * TILE, (last + block_e) // 2 // TILE * TILE
    units = up.shape[1]
    gain_two = ln2_gain.reshape(1, width)

    def picked(chunks, pieces):
        lists = pieces if isinstance(pieces[0], list) else [pieces]
        used = sorted({p[0] for some in lists for p in some})
        moved = [[(used.index(p[0]), *p[1:]) for p in some] for some in lists]
        return [chunks[i].array for i in used], moved if isinstance(pieces[0], list) else moved[0]

    if dims == (4, 2, 2) and block % (2 * TILE) == 0 and block_e % TILE == 0 and units % columns == 0:
        spans = ((0, cut), (cut, last), (block_e, far_cut), (far_cut, last), (0, block_e), (0, far_cut))
        work = Gather(*pack(shards, up, down), spans, dims)
        work.slot(0)
        picture, pos, gain_one = work.end_slot(picture, pos, gain_one)
        work.slot(1)
        picture, pos, gain_one = work.end_slot(picture, pos, gain_one)
        work.slot(2)
        other_picture = swap_columns(picture)
        other_picture, picture = work.end_slot(other_picture, picture)
        work.slot(3)
        other_picture, picture = work.end_slot(other_picture, picture)
        chunks, own_pieces = picked(work.early, pieces_of(work.early, spans, (0, block_e)))
        work.slot(4)
        mine = embed(pos, dims, picture, other_picture, chunks, own_pieces, block_e, columns)
        del work.early
        (mine,) = work.end_slot(mine)
        pieces = [pieces_of(work.parts, spans, (bounds[i], bounds[i + 1])) for i in range(5)]
        work.slot(5)
        recv = swap_columns(mine)
        chunks, own_pieces = picked(work.parts, pieces[1:4])
        q, k, v = project(pos, dims, mine, recv, gain_one, chunks, own_pieces, block, width)
        chunks, own_pieces = picked(work.parts, pieces[4])
        keep, send = attention(pos, dims, q, k, v, chunks, own_pieces, block, width)
        mine, recv, keep, send = work.end_slot(mine, recv, keep, send)
        work.slot(6)
        came = swap_columns(send)
        residual, normed = residual_and_norm(pos, mine, recv, keep, came, gain_two)
        residual, normed = work.end_slot(residual, normed)
        work.slot(7)
        normed_came = swap_columns(normed)
        up_pieces = wide_pieces(work.up_parts, block // 2, columns)
        hidden = up_layer(
            pos, dims, normed, normed_came, [c.array for c in work.up_parts], up_pieces, block, units
        )
        residual, hidden = work.end_slot(residual, hidden)
        work.slot(8)
        starts = []

        def down_part(part):
            own_pieces = wide_pieces(part, block // 2, columns)
            spots = sorted({p[3][0] for p in own_pieces})
            starts.append(spots)
            size = width // dims[0] * len(spots)
            return down_layer(
                pos, dims, hidden, [c.array for c in part], own_pieces, block, spots[0], size
            )

        kept, sent = down_part(work.down_parts[0])
        kept, sent, residual, hidden = work.end_slot(kept, sent, residual, hidden)
        finals = [kept, swap_columns(sent)]
        kept, sent = down_part(work.down_parts[1])
        last = [kept, swap_columns(sent)]
    else:
        *w_three, w_last = [
            lax.all_gather(s, "dp", axis=0, tiled=True)
            for s in (embed_weight, w_qkv[0], w_qkv[1], w_qkv[2], w_out.T, up, down)
        ]
        one = lambda w: [(0, 0, w.shape[0], None, 0)]
        mine = embed(
            pos, dims, picture, swap_columns(picture), w_three[:1], one(w_three[0]), block_e, columns
        )
        recv = swap_columns(mine)
        some = [[(i, 0, w.shape[0], None, 0)] for i, w in enumerate(w_three[1:4])]
        q, k, v = project(pos, dims, mine, recv, gain_one, w_three[1:4], some, block, width)
        keep, send = attention(pos, dims, q, k, v, [w_three[4]], one(w_three[4]), block, width)
        came = swap_columns(send)
        residual, normed = residual_and_norm(pos, mine, recv, keep, came, gain_two)
        hidden = up_layer(
            pos, dims, normed, swap_columns(normed), [w_three[5]], one(w_three[5]), block, units
        )
        kept, sent = down_layer(pos, dims, hidden, [w_last], one(w_last), block, None, width)
        finals, starts, last = [], [[None]], [kept, swap_columns(sent)]
    wanted = targets[0]
    if finals:
        encoded, squares = output_layer(pos, residual, wanted, dims[0], starts[:-1], finals)
    else:
        encoded, squares = jnp.zeros_like(wanted), jnp.zeros((8, 128), jnp.float32)
    encoded, sums = output_layer(
        pos,
        residual,
        wanted,
        dims[0],
        starts[-1:],
        last,
        (encoded, squares),
        devices * cores,
    )
    sums = lax.all_to_all(sums, ("dp", "mp"), 0, 0, tiled=True)
    total_squares, total_number = jnp.sum(sums, axis=(0, 1))
    return (encoded[None], total_squares / (width * total_number))


def solution(mesh):
    in_specs = (
        P(("dp", "mp"), None, None),
        P("dp", None),
        P("dp", None),
        P("dp", "mp"),
        P(None, "dp", "mp"),
        P("mp", "dp"),
        P("dp", "mp"),
        P("mp", "dp"),
        P(),
        P(),
        P("dp", None, "mp", None),
    )
    out_specs = (P("dp", None, "mp", None), P())
    return jax.shard_map(
        on_device, mesh=mesh, in_specs=in_specs, out_specs=out_specs, check_vma=False
    )
```

```python
import functools

import jax
import jax.numpy as jnp
from jax import lax
from jax.experimental import pallas as pl
from jax.experimental.pallas import tpu as pltpu
from jax.sharding import PartitionSpec as P

HEAD = 64
TILE = 16
SPARE = 8
Z, Y, X = 0, 1, 2
MIB = 1 << 20
POS_Z, POS_Y, POS_X, POS_M, POS_LEN, POS_STEP = 0, 1, 2, 3, 4, 6


def ring_dims(count):
    nz = 4 if count % 4 == 0 else 1
    nx = 1
    while nx * nx < count // nz:
        nx *= 2
    ny = count // nz // nx
    return (nz, ny, nx) if nz * ny * nx == count else (1, 1, count)


def shift(value, dims, *axes):
    pairs = []
    for z in range(dims[0]):
        for y in range(dims[1]):
            for x in range(dims[2]):
                to = [z, y, x]
                for axis in axes:
                    to[axis] = (to[axis] + 1) % dims[axis]
                pairs.append(
                    ((z * dims[1] + y) * dims[2] + x, (to[0] * dims[1] + to[1]) * dims[2] + to[2])
                )
    return lax.ppermute(value, "dp", pairs)


class Chunk:
    def __init__(self, array, slots, half, rows, base=0):
        self.array, self.slots, self.half, self.rows, self.base = array, slots, half, rows, base

    def moved(self, array, axis):
        slots = [tuple(v + (i == axis) for i, v in enumerate(s)) for s in self.slots]
        return Chunk(array, slots, self.half, self.rows, self.base)

    def block(self, i, first=0, last=None):
        last = self.rows if last is None else last
        return (self.array, self.base + i * self.rows + first, last - first)

    def all(self, first=0, last=None):
        return [self.block(i, first, last) for i in range(len(self.slots))]


def stack_kernel(plan, *refs):
    sources, results = refs[: -len(plan)], refs[-len(plan) :]
    for result, taken in zip(results, plan, strict=True):
        at = 0
        for number, row, rows in taken:
            result[pl.ds(at, rows), :] = sources[number][pl.ds(row, rows), :]
            at += rows


def stack(*results):
    sources = []
    for taken in results:
        for array, _, _ in taken:
            if all(array is not other for other in sources):
                sources.append(array)

    def number(array):
        return next(i for i, other in enumerate(sources) if other is array)

    plan = [[(number(array), row, rows) for array, row, rows in taken] for taken in results]
    return pl.pallas_call(
        functools.partial(stack_kernel, plan),
        out_shape=tuple(
            jax.ShapeDtypeStruct((sum(rows for _, _, rows in taken), taken[0][0].shape[1]), taken[0][0].dtype)
            for taken in results
        ),
        in_specs=[vmem_spec()] * len(sources),
        out_specs=(vmem_spec(),) * len(results),
        compiler_params=limits(8),
        cost_estimate=cost(0, 2 * MIB),
        name="stack",
    )(*sources)


def swap_columns(value):
    return lax.ppermute(value, "mp", [(0, 1), (1, 0)])


class Gather:
    def __init__(self, first, side_a, side_b, spans, dims):
        self.dims, self.spans, self.half = dims, spans, side_a.shape[0] // 2
        self.first, self.side_a, self.side_b = first, side_a, side_b

    def move(self, value, axis):
        return shift(value, self.dims, axis)

    def step(self, chunk, axis):
        return chunk.moved(shift(chunk.array, self.dims, axis), axis)

    def ends(self, low, kind):
        first, last = self.spans[kind]
        return [(v, first, last - first) for v in self.first_z[low : low + 2]]

    def chunk(self, array, slots, kind):
        return Chunk(array, slots, kind, self.spans[kind][1] - self.spans[kind][0])

    def both(self, a, b):
        return [a, self.step(a, Y), b, self.step(b, X)]

    def last(self, first, second):
        a, b = stack(sum((c.all() for c in first), []), sum((c.all() for c in second), []))
        a = Chunk(a, sum((c.slots for c in first), []), 0, self.half)
        b = Chunk(b, sum((c.slots for c in second), []), 1, self.half)
        return self.both(a, b)

    def own_halves(self, k):
        rows = (k * self.half, self.half)
        return ([(self.side_a, *rows), (self.from_x, *rows)], [(self.side_b, *rows), (self.from_y, *rows)])

    def pair(self, b, a):
        (value,) = stack(b.all() + a.all() + [a.block(0, 0, SPARE)])
        return value

    def pair_moved(self, value, b, a):
        value = self.move(value, Z)
        b, a = b.moved(value, Z), a.moved(value, Z)
        b.base, a.base = 0, 2 * self.half
        return b, a, value

    def slot(self, number):
        if number == 0:
            self.first_z = [self.first, self.move(self.first, Z)]
            self.from_x, self.from_y = self.move(self.side_a, X), self.move(self.side_b, Y)
        elif number == 1:
            self.first_z.append(self.move(self.first_z[-1], Z))
            near = [(0, 0, 0), (1, 0, 0)]
            a, *b = stack(self.ends(0, 0), self.ends(0, 1)[:1], self.ends(0, 1)[1:])
            self.a = self.chunk(a, near, 0)
            self.b = [self.chunk(v, near[i : i + 1], 1) for i, v in enumerate(b)]
            self.a_far, self.b_far = self.step(self.a, X), [self.step(c, Y) for c in self.b]
            made = stack(*self.own_halves(0), *self.own_halves(1))
            along_x, along_y = [(0, 0, 0), (0, 0, 1)], [(0, 0, 0), (0, 1, 0)]
            self.up_a, self.down_a = ([Chunk(v, along_x, 0, self.half)] for v in made[0::2])
            self.up_b, self.down_b = ([Chunk(v, along_y, 1, self.half)] for v in made[1::2])
        elif number == 2:
            self.first_z.append(self.move(self.first_z[-1], Z))
            del self.side_a, self.side_b, self.from_x, self.from_y
            from_b = self.b + self.b_far
            a, b = stack(self.a.all() + self.a_far.all(), sum((c.all() for c in from_b), []))
            self.a = self.chunk(a, self.a.slots + self.a_far.slots, 0)
            self.b = self.chunk(b, sum((c.slots for c in from_b), []), 1)
            self.parts = self.both(self.a, self.b)
            self.up_a.append(self.step(self.up_a[0], Z))
        elif number == 3:
            value = self.pair(self.up_b[0], self.up_a[1])
            b, a, self.z_pair = self.pair_moved(value, self.up_b[0], self.up_a[1])
            self.up_b.append(b)
            self.up_a.append(a)
            far = [(2, 0, 0), (3, 0, 0)]
            a, b, own = stack(self.ends(2, 5), self.ends(2, 3) + self.ends(2, 4), self.ends(2, 4))
            self.a, self.b = self.chunk(a, far, 5), self.chunk(b, far, 3)
            self.a_far, self.b_far = self.step(self.a, X), self.step(self.b, Y)
            corner = self.chunk(shift(own, self.dims, X, Y), [(2, 1, 1), (3, 1, 1)], 4)
            own_far = self.chunk(self.b_far.array, [(2, 1, 0), (3, 1, 0)], 4)
            own_far.base = 2 * self.b.rows
            self.early = self.parts[:2] + [self.a, self.a_far, own_far, corner]
        elif number == 4:
            b, a, self.z_pair = self.pair_moved(self.z_pair, self.up_b[1], self.up_a[2])
            self.up_b.append(b)
            self.up_a.append(a)
            first = self.spans[2][0] - self.spans[5][0]
            a, b = stack(self.a.all(first) + self.a_far.all(first), self.b.all() + self.b_far.all())
            self.a = self.chunk(a, self.a.slots + self.a_far.slots, 2)
            self.b = self.chunk(b, self.b.slots + self.b_far.slots, 3)
            self.parts += self.both(self.a, self.b)
        elif number == 5:
            value = self.pair(self.up_b[2], self.down_a[0])
            b, a, self.z_pair = self.pair_moved(value, self.up_b[2], self.down_a[0])
            self.up_parts = self.last(self.up_a[:2], self.up_b[:2])
            self.up_b.append(b)
            self.down_a.append(a)
        elif number == 6:
            value = self.pair(self.down_b[0], self.down_a[1])
            b, a, self.z_pair = self.pair_moved(value, self.down_b[0], self.down_a[1])
            self.up_parts += self.last(self.up_a[2:], self.up_b[2:])
            self.down_b.append(b)
            self.down_a.append(a)
        elif number == 7:
            b, a, self.z_pair = self.pair_moved(self.z_pair, self.down_b[1], self.down_a[2])
            self.down_parts = [self.last(self.down_a[:2], self.down_b[:2])]
            self.down_b.append(b)
            self.down_a.append(a)
        elif number == 8:
            del self.z_pair
            far_a, far_b = self.down_a[2:], self.down_b[2]
            value, near = stack(*(c.all() + [c.block(0, 0, SPARE)] for c in (far_b, far_a[0])))
            ahead, near = Chunk(value, far_b.slots, 1, self.half), Chunk(near, far_a[0].slots, 0, self.half)
            corner = ahead.moved(shift(value, self.dims, Z, X), Z)
            corner = corner.moved(corner.array, X)
            near_far = self.step(near, Y)
            b, a = stack(far_b.all(), far_a[1].all())
            b, a = Chunk(b, far_b.slots, 1, self.half), Chunk(a, far_a[1].slots, 0, self.half)
            self.down_parts.append(
                [near, near_far, b, self.step(b, X), a, self.step(a, Y), self.step(b, Z), corner]
            )

    def end_slot(self, *others):
        chunks, arrays = [], []
        for name, value in vars(self).items():
            for i, v in enumerate(value if isinstance(value, list) else [value]):
                for k, w in enumerate(v if isinstance(v, list) else [v]):
                    if isinstance(w, Chunk):
                        if all(w is not c for c in chunks):
                            chunks.append(w)
                    elif isinstance(w, jax.Array):
                        arrays.append((name, i, w))
        held = []
        for c in chunks:
            if all(c.array is not w for w in held):
                held.append(c.array)
        together = lax.optimization_barrier((tuple(held), tuple(w for _, _, w in arrays), others))
        for c in chunks:
            c.array = together[0][next(i for i, w in enumerate(held) if w is c.array)]
        for (name, i, _), new in zip(arrays, together[1], strict=True):
            if isinstance(vars(self)[name], list):
                vars(self)[name][i] = new
            else:
                setattr(self, name, new)
        return together[2]


def pieces_of(chunks, spans, segment):
    found = []
    for number, chunk in enumerate(chunks):
        first, last = spans[chunk.half]
        low, high = max(first, segment[0]), min(last, segment[1])
        if low < high:
            for i, slot in enumerate(chunk.slots):
                row = chunk.base + i * chunk.rows + low - first
                found.append((number, row, high - low, slot, low - segment[0]))
    return found


def wide_pieces(chunks, half, width):
    found = []
    for number, chunk in enumerate(chunks):
        for i, slot in enumerate(chunk.slots):
            for c in range(chunk.rows // half):
                row = chunk.base + i * chunk.rows + c * half
                found.append((number, row, half, slot, chunk.half * half, c * width))
    return found


def source(pos, slot, dims, z_first=None):
    z, y, x = (lax.rem(pos[i] - slot[i] + dims[i], dims[i]) for i in (0, 1, 2))
    if z_first is not None:
        z = slot[0] - z_first
    return (z * dims[1] + y) * dims[2] + x


def lay_out(pos, dims, refs, pieces, into, block, z_first=None):
    for number, row, rows, slot, offset, *column in pieces:
        to = offset
        if slot is not None:
            to = pl.multiple_of(source(pos, slot, dims, z_first) * block + offset, TILE)
        first, width = (column[0] if column else 0), refs[number].shape[1]
        into[pl.ds(to, rows), first : first + width] = refs[number][pl.ds(row, rows), :]


def nt_dot(left, right):
    return lax.dot_general(left, right, (((1,), (1,)), ((), ())), preferred_element_type=jnp.float32)


def dot(left, right):
    return jnp.dot(left, right, preferred_element_type=jnp.float32)


def any_spec():
    return pl.BlockSpec(memory_space=pl.ANY)


def hbm_spec():
    return pl.BlockSpec(memory_space=pltpu.HBM)


def vmem_spec():
    return pl.BlockSpec(memory_space=pltpu.VMEM)


def smem_spec():
    return pl.BlockSpec(memory_space=pltpu.SMEM)


def limits(mib):
    return pltpu.CompilerParams(vmem_limit_bytes=mib * MIB)


def cost(flops, moved, exps=0):
    return pl.CostEstimate(flops=0, bytes_accessed=1024, transcendentals=0)


def pack_kernel(*rest):
    *shards, up, down, first, side_a, side_b, sems = rest
    half, width = up.shape[0] // 2, first.shape[1]
    wide = up.shape[1] // width
    moves, at = [], 0
    for shard in shards:
        for part in [shard] if len(shard.shape) == 2 else [shard.at[i] for i in range(shard.shape[0])]:
            moves.append((part, first.at[pl.ds(at, part.shape[0])]))
            at += part.shape[0]
    for k, shard in enumerate((up, down)):
        for c in range(wide):
            to, columns = pl.ds((k * wide + c) * half, half), pl.ds(c * width, width)
            moves.append((shard.at[pl.ds(0, half), columns], side_a.at[to]))
            moves.append((shard.at[pl.ds(half, half), columns], side_b.at[to]))
    made = [pltpu.make_async_copy(a, b, sems.at[i]) for i, (a, b) in enumerate(moves)]
    for c in made:
        c.start()
    for c in made:
        c.wait()


def pack(shards, up, down):
    rows = sum(s.size for s in shards) // shards[0].shape[1]
    first = jax.ShapeDtypeStruct((rows, shards[0].shape[1]), up.dtype)
    wide = up.shape[1] // shards[0].shape[1]
    side = jax.ShapeDtypeStruct((up.shape[0] * wide, shards[0].shape[1]), up.dtype)
    return pl.pallas_call(
        pack_kernel,
        out_shape=(first, side, side),
        in_specs=[hbm_spec()] * (len(shards) + 2),
        out_specs=(vmem_spec(),) * 3,
        scratch_shapes=[pltpu.SemaphoreType.DMA((len(shards) + 2 + 4 * wide,))],
        compiler_params=limits(60),
        cost_estimate=cost(0, 2 * MIB),
        name="pack",
    )(*shards, up, down)


def embed_kernel(n, dims, pieces, block, pos, mine, other, *rest):
    refs, (tokens, weight) = rest[:n], rest[n:]
    lay_out(pos, dims, refs, pieces, weight, block)
    tokens[0] = dot(mine[...], weight[...]).astype(tokens.dtype)
    tokens[1] = dot(other[...], weight[...]).astype(tokens.dtype)


def embed(pos, dims, mine, other, chunks, pieces, block, columns):
    patches, pixels = mine.shape
    n = len(chunks)
    return pl.pallas_call(
        functools.partial(embed_kernel, n, dims, pieces, block),
        out_shape=jax.ShapeDtypeStruct((2, patches, columns), mine.dtype),
        in_specs=[smem_spec(), vmem_spec(), vmem_spec()] + [vmem_spec()] * n,
        out_specs=vmem_spec(),
        scratch_shapes=[pltpu.VMEM((pixels, columns), mine.dtype)],
        compiler_params=limits(8),
        cost_estimate=cost(4 * patches * pixels * columns, 4 * MIB),
        name="embed",
    )(pos, mine, other, *chunks)


def project_kernel(n, dims, pieces, block, pos, mine, recv, gain, *rest):
    refs = rest[:n]
    q, k, v, weight, normed = rest[n:]
    m = pos[POS_M]
    columns = mine.shape[2]
    width = 2 * columns
    for i in range(2):
        low = mine[i].astype(jnp.float32)
        high = recv[1 - i].astype(jnp.float32)
        average = (
            jnp.sum(low, axis=-1, keepdims=True) + jnp.sum(high, axis=-1, keepdims=True)
        ) / width
        low, high = low - average, high - average
        spread = (
            jnp.sum(low * low, axis=-1, keepdims=True) + jnp.sum(high * high, axis=-1, keepdims=True)
        ) / width
        scale = lax.rsqrt(spread + 1e-06)
        normed[i, 0] = (low * scale * gain[0:1]).astype(normed.dtype)
        normed[i, 1] = (high * scale * gain[1:2]).astype(normed.dtype)
    here = pl.ds(pl.multiple_of(m * columns, columns), columns)
    there = pl.ds(pl.multiple_of((1 - m) * columns, columns), columns)
    for some, result, factor in zip(pieces, (q, k, v), (HEAD**-0.5, 1.0, 1.0), strict=True):
        lay_out(pos, dims, refs, some, weight, block)
        for i in range(2):
            value = dot(normed[i, 0], weight[here, :]) + dot(normed[i, 1], weight[there, :])
            if factor != 1.0:
                value = value * factor
            result[i] = value.astype(result.dtype)


def project(pos, dims, mine, recv, gain, chunks, pieces, block, width):
    _, patches, columns = mine.shape
    n = len(chunks)
    kind = mine.dtype
    out = jax.ShapeDtypeStruct(mine.shape, kind)
    return pl.pallas_call(
        functools.partial(project_kernel, n, dims, pieces, block),
        out_shape=(out, out, out),
        in_specs=[smem_spec(), vmem_spec(), vmem_spec(), vmem_spec()] + [vmem_spec()] * n,
        out_specs=(vmem_spec(),) * 3,
        scratch_shapes=[
            pltpu.VMEM((width, columns), kind),
            pltpu.VMEM((2, 2, patches, columns), kind),
        ],
        compiler_params=limits(11),
        cost_estimate=cost(2 * 2 * patches * width * columns * 3, 8 * MIB),
        name="project",
    )(pos, mine, recv, gain, *chunks)


def attention_kernel(n, dims, pieces, block, pos, q, k, v, *rest):
    refs = rest[:n]
    keep, send, wo, mixed = rest[n:]
    lay_out(pos, dims, refs, pieces, wo, block)
    m = pos[POS_M]
    patches, columns = q.shape[1:]
    rows_own = patches // 2
    pair = 2 * HEAD
    key_ids = lax.broadcasted_iota(jnp.int32, (1, patches), 1)
    lane = lax.broadcasted_iota(jnp.int32, (patches, pair), 1)
    first = lane < HEAD
    for i in range(2):
        masked = jnp.where(key_ids < pos[POS_LEN + i], 0.0, -1e30).astype(jnp.float32)
        for h in range(columns // pair):
            cut = slice(h * pair, (h + 1) * pair)
            q_pair, k_pair, v_pair = q[i, :, cut], k[i, :, cut], v[i, :, cut]
            found = []
            for own in (first, jnp.logical_not(first)):
                scores = nt_dot(q_pair, jnp.where(own, k_pair, jnp.zeros_like(k_pair))) + masked
                expo = jnp.exp(scores - jnp.max(scores, axis=-1, keepdims=True))
                value = dot(
                    expo.astype(v_pair.dtype), jnp.where(own, v_pair, jnp.ones_like(v_pair))
                )
                found.append(value / pltpu.roll(value, HEAD, 1))
            mixed[i, :, cut] = jnp.where(first, found[0], found[1]).astype(mixed.dtype)
    own_rows = pl.ds(pl.multiple_of(m * rows_own, rows_own), rows_own)
    far_rows = pl.ds(pl.multiple_of((1 - m) * rows_own, rows_own), rows_own)
    for i in range(2):
        keep[i] = nt_dot(mixed[i, own_rows, :], wo[...]).astype(keep.dtype)
        send[i] = nt_dot(mixed[i, far_rows, :], wo[...]).astype(send.dtype)


def attention(pos, dims, q, k, v, chunks, pieces, block, width):
    _, patches, columns = q.shape
    n = len(chunks)
    out = jax.ShapeDtypeStruct((2, patches // 2, width), q.dtype)
    return pl.pallas_call(
        functools.partial(attention_kernel, n, dims, pieces, block),
        out_shape=(out, out),
        in_specs=[smem_spec()] + [vmem_spec()] * 3 + [vmem_spec()] * n,
        out_specs=(vmem_spec(), vmem_spec()),
        scratch_shapes=[
            pltpu.VMEM((width, columns), q.dtype),
            pltpu.VMEM(q.shape, q.dtype),
        ],
        compiler_params=limits(10),
        cost_estimate=cost(
            4 * patches * width * columns + 8 * patches * patches * columns,
            8 * MIB,
            2 * patches * patches * columns // HEAD,
        ),
        name="attention",
    )(pos, q, k, v, *chunks)


def residual_kernel(pos, mine, recv, keep, came, gain, residual, normed):
    m = pos[POS_M]
    columns = mine.shape[2]
    rows = keep.shape[1]
    width = 2 * columns
    own_rows = pl.ds(pl.multiple_of(m * rows, rows), rows)
    here = pl.ds(pl.multiple_of(m * columns, columns), columns)
    there = pl.ds(pl.multiple_of((1 - m) * columns, columns), columns)
    for i in range(2):
        parts = []
        for tokens, at in ((mine[i, own_rows, :], here), (recv[1 - i, own_rows, :], there)):
            parts.append(
                tokens.astype(jnp.float32)
                + (keep[i, :, at].astype(jnp.float32) + came[1 - i, :, at].astype(jnp.float32))
            )
            residual[i, :, at] = parts[-1]
        average = sum(jnp.sum(v, axis=-1, keepdims=True) for v in parts) / width
        parts = [v - average for v in parts]
        spread = sum(jnp.sum(v * v, axis=-1, keepdims=True) for v in parts) / width
        scale = lax.rsqrt(spread + 1e-06)
        for v, at in zip(parts, (here, there), strict=True):
            normed[i, :, at] = (v * scale * gain[0:1, at]).astype(normed.dtype)


def residual_and_norm(pos, mine, recv, keep, came, gain):
    return pl.pallas_call(
        residual_kernel,
        out_shape=(
            jax.ShapeDtypeStruct(keep.shape, jnp.float32),
            jax.ShapeDtypeStruct(keep.shape, keep.dtype),
        ),
        in_specs=[smem_spec()] + [vmem_spec()] * 5,
        out_specs=(vmem_spec(), vmem_spec()),
        compiler_params=limits(8),
        cost_estimate=cost(10 * keep.size, 10 * MIB),
        name="residual",
    )(pos, mine, recv, keep, came, gain)


def gelu(x):
    return x * (0.5 * lax.erf(x * 0.7071067811865476) + 0.5)


def up_kernel(n, dims, pieces, block, pos, own, came, *rest):
    refs, (hidden, weight) = rest[:n], rest[n:]
    lay_out(pos, dims, refs, pieces, weight, block)
    tile = 512
    rows, width = own.shape[1:]
    for k, side in enumerate((own, came)):
        left = side[...].reshape(2 * rows, width)
        for j in range(hidden.shape[-1] // tile):
            at = slice(j * tile, (j + 1) * tile)
            value = gelu(dot(left, weight[:, at])).astype(hidden.dtype).reshape(2, rows, tile)
            if k == 0:
                hidden[0, :, :, at] = value
            else:
                hidden[1, 0, :, at] = value[1]
                hidden[1, 1, :, at] = value[0]


def up_layer(pos, dims, own, came, chunks, pieces, block, units):
    _, rows, width = own.shape
    n = len(chunks)
    return pl.pallas_call(
        functools.partial(up_kernel, n, dims, pieces, block),
        out_shape=jax.ShapeDtypeStruct((2, 2, rows, units), own.dtype),
        in_specs=[smem_spec(), vmem_spec(), vmem_spec()] + [vmem_spec()] * n,
        out_specs=vmem_spec(),
        scratch_shapes=[pltpu.VMEM((width, units), own.dtype)],
        compiler_params=limits(12),
        cost_estimate=cost(8 * rows * width * units, 10 * MIB, 4 * rows * units),
        name="up",
    )(pos, own, came, *chunks)


def down_kernel(n, dims, pieces, block, z_first, pos, hidden, *rest):
    refs, (keep, send, weight) = rest[:n], rest[n:]
    lay_out(pos, dims, refs, pieces, weight, block, z_first)
    for k, result in enumerate((keep, send)):
        left = hidden[k].reshape(-1, hidden.shape[-1])
        result[...] = nt_dot(left, weight[...]).astype(result.dtype).reshape(result.shape)


def down_layer(pos, dims, hidden, chunks, pieces, block, z_first, columns):
    _, _, rows, units = hidden.shape
    n = len(chunks)
    out = jax.ShapeDtypeStruct((2, rows, columns), hidden.dtype)
    return pl.pallas_call(
        functools.partial(down_kernel, n, dims, pieces, block, z_first),
        out_shape=(out, out),
        in_specs=[smem_spec(), vmem_spec()] + [vmem_spec()] * n,
        out_specs=(vmem_spec(), vmem_spec()),
        scratch_shapes=[pltpu.VMEM((columns, units), hidden.dtype)],
        compiler_params=limits(8),
        cost_estimate=cost(8 * rows * columns * units, 8 * MIB),
        name="down",
    )(pos, hidden, *chunks)


def output_kernel(n, nz, starts, ending, pos, residual, targets, *rest):
    parts, (encoded, sums) = rest[:n], rest[-2:]
    m = pos[POS_M]
    rows = residual.shape[1]
    total = jnp.zeros((), jnp.float32)
    row_ids = m * rows + lax.broadcasted_iota(jnp.int32, (rows, 1), 0)
    if ending:
        before, total_before = rest[n : n + 2]
        encoded[...] = before[...]
        number = (pos[POS_LEN] + pos[POS_LEN + 1]).astype(jnp.float32) * 0.5
        total = total_before[0, 0]
    for i in range(2):
        s = pos[POS_STEP] if i == 0 else 1 - pos[POS_STEP]
        usable = row_ids < pos[POS_LEN + i]
        found = jnp.zeros((rows, 1), jnp.float32)
        for j, spots in enumerate(starts):
            keep, came = parts[2 * j], parts[2 * j + 1]
            size = keep.shape[2] // len(spots)
            for b, back in enumerate(spots):
                at = slice(b * size, (b + 1) * size)
                if back is None:
                    place = pl.ds(0, size)
                else:
                    begin = lax.rem(pos[POS_Z] - back + nz, nz) * size
                    place = pl.ds(pl.multiple_of(begin, size), size)
                value = residual[i, :, place] + (
                    keep[i, :, at].astype(jnp.float32) + came[1 - i, :, at].astype(jnp.float32)
                )
                encoded[s, :, place] = value.astype(encoded.dtype)
                misfit = value - targets[s, :, place].astype(jnp.float32)
                found = found + jnp.sum(misfit * misfit, axis=-1, keepdims=True)
        total = total + jnp.sum(jnp.where(usable, found, 0.0))
    if ending:
        lane = lax.broadcasted_iota(jnp.int32, sums.shape, 2)
        sums[...] = jnp.where(lane == 0, total, number)
    else:
        sums[...] = jnp.full(sums.shape, total, jnp.float32)


def output_layer(pos, residual, targets, nz, starts, parts, ending=(), devices=0):
    sums = (devices, 1, 2) if ending else (8, 128)
    specs = [vmem_spec(), vmem_spec()] if ending else []
    return pl.pallas_call(
        functools.partial(output_kernel, len(parts), nz, starts, bool(ending)),
        out_shape=(
            jax.ShapeDtypeStruct(residual.shape, targets.dtype),
            jax.ShapeDtypeStruct(sums, jnp.float32),
        ),
        in_specs=[smem_spec()] + [vmem_spec()] * (2 + len(parts)) + specs,
        out_specs=(vmem_spec(), vmem_spec()),
        compiler_params=limits(8),
        cost_estimate=cost(8 * residual.size, 8 * MIB),
        name="output",
    )(pos, residual, targets, *parts, *ending)


def on_device(
    pixels, counts, owner, embed_weight, w_qkv, w_out, w_up, w_down, ln1_gain, ln2_gain, targets
):
    picture = pixels[0]
    devices, cores = lax.axis_size("dp"), lax.axis_size("mp")
    assert cores == 2
    index, m = lax.axis_index("dp"), lax.axis_index("mp")
    dims = ring_dims(devices)
    width = ln1_gain.shape[0]
    columns = width // cores
    lengths, order = counts[0], owner[0]
    length_mine = jnp.where(m == 0, lengths[0], lengths[1])
    length_other = jnp.where(m == 0, lengths[1], lengths[0])
    step_mine = jnp.where(order[0] == m, 0, 1)
    pos = jnp.stack(
        [
            index // (dims[1] * dims[2]),
            index // dims[2] % dims[1],
            index % dims[2],
            m,
            length_mine,
            length_other,
            step_mine,
            jnp.zeros_like(m),
        ]
    ).astype(jnp.int32)
    gain_halves = ln1_gain.reshape(cores, columns)
    gain_one = jnp.where(m == 0, gain_halves, gain_halves[::-1])

    shards = [embed_weight, w_qkv, w_out.T]
    up, down = w_up, w_down.T
    block, block_e = up.shape[0], embed_weight.shape[0]
    bounds = [0, block_e] + [block_e + (i + 1) * block for i in range(4)]
    last = bounds[-1]
    cut, far_cut = last // 2 // TILE * TILE, (last + block_e) // 2 // TILE * TILE
    units = up.shape[1]
    gain_two = ln2_gain.reshape(1, width)

    def picked(chunks, pieces):
        lists = pieces if isinstance(pieces[0], list) else [pieces]
        used = sorted({p[0] for some in lists for p in some})
        moved = [[(used.index(p[0]), *p[1:]) for p in some] for some in lists]
        return [chunks[i].array for i in used], moved if isinstance(pieces[0], list) else moved[0]

    if dims == (4, 2, 2) and block % (2 * TILE) == 0 and block_e % TILE == 0 and units % columns == 0:
        spans = ((0, cut), (cut, last), (block_e, far_cut), (far_cut, last), (0, block_e), (0, far_cut))
        work = Gather(*pack(shards, up, down), spans, dims)
        work.slot(0)
        other_picture = swap_columns(picture)
        other_picture, picture, pos, gain_one = work.end_slot(other_picture, picture, pos, gain_one)
        work.slot(1)
        other_picture, picture, pos, gain_one = work.end_slot(other_picture, picture, pos, gain_one)
        work.slot(2)
        other_picture, picture = work.end_slot(other_picture, picture)
        work.slot(3)
        other_picture, picture = work.end_slot(other_picture, picture)
        chunks, own_pieces = picked(work.early, pieces_of(work.early, spans, (0, block_e)))
        work.slot(4)
        mine = embed(pos, dims, picture, other_picture, chunks, own_pieces, block_e, columns)
        del work.early
        (mine,) = work.end_slot(mine)
        pieces = [pieces_of(work.parts, spans, (bounds[i], bounds[i + 1])) for i in range(5)]
        work.slot(5)
        recv = swap_columns(mine)
        chunks, own_pieces = picked(work.parts, pieces[1:4])
        q, k, v = project(pos, dims, mine, recv, gain_one, chunks, own_pieces, block, width)
        chunks, own_pieces = picked(work.parts, pieces[4])
        keep, send = attention(pos, dims, q, k, v, chunks, own_pieces, block, width)
        mine, recv, keep, send = work.end_slot(mine, recv, keep, send)
        work.slot(6)
        came = swap_columns(send)
        residual, normed = residual_and_norm(pos, mine, recv, keep, came, gain_two)
        residual, normed = work.end_slot(residual, normed)
        work.slot(7)
        normed_came = swap_columns(normed)
        up_pieces = wide_pieces(work.up_parts, block // 2, columns)
        hidden = up_layer(
            pos, dims, normed, normed_came, [c.array for c in work.up_parts], up_pieces, block, units
        )
        residual, hidden = work.end_slot(residual, hidden)
        work.slot(8)
        starts = []

        def down_part(part):
            own_pieces = wide_pieces(part, block // 2, columns)
            spots = sorted({p[3][0] for p in own_pieces})
            starts.append(spots)
            size = width // dims[0] * len(spots)
            return down_layer(
                pos, dims, hidden, [c.array for c in part], own_pieces, block, spots[0], size
            )

        kept, sent = down_part(work.down_parts[0])
        kept, sent, residual, hidden = work.end_slot(kept, sent, residual, hidden)
        finals = [kept, swap_columns(sent)]
        kept, sent = down_part(work.down_parts[1])
        last = [kept, swap_columns(sent)]
    else:
        *w_three, w_last = [
            lax.all_gather(s, "dp", axis=0, tiled=True)
            for s in (embed_weight, w_qkv[0], w_qkv[1], w_qkv[2], w_out.T, up, down)
        ]
        one = lambda w: [(0, 0, w.shape[0], None, 0)]
        mine = embed(
            pos, dims, picture, swap_columns(picture), w_three[:1], one(w_three[0]), block_e, columns
        )
        recv = swap_columns(mine)
        some = [[(i, 0, w.shape[0], None, 0)] for i, w in enumerate(w_three[1:4])]
        q, k, v = project(pos, dims, mine, recv, gain_one, w_three[1:4], some, block, width)
        keep, send = attention(pos, dims, q, k, v, [w_three[4]], one(w_three[4]), block, width)
        came = swap_columns(send)
        residual, normed = residual_and_norm(pos, mine, recv, keep, came, gain_two)
        hidden = up_layer(
            pos, dims, normed, swap_columns(normed), [w_three[5]], one(w_three[5]), block, units
        )
        kept, sent = down_layer(pos, dims, hidden, [w_last], one(w_last), block, None, width)
        finals, starts, last = [], [[None]], [kept, swap_columns(sent)]
    wanted = targets[0]
    if finals:
        encoded, squares = output_layer(pos, residual, wanted, dims[0], starts[:-1], finals)
    else:
        encoded, squares = jnp.zeros_like(wanted), jnp.zeros((8, 128), jnp.float32)
    encoded, sums = output_layer(
        pos,
        residual,
        wanted,
        dims[0],
        starts[-1:],
        last,
        (encoded, squares),
        devices * cores,
    )
    sums = lax.all_to_all(sums, ("dp", "mp"), 0, 0, tiled=True)
    total_squares, total_number = jnp.sum(sums, axis=(0, 1))
    return (encoded[None], total_squares / (width * total_number))


def solution(mesh):
    in_specs = (
        P(("dp", "mp"), None, None),
        P("dp", None),
        P("dp", None),
        P("dp", "mp"),
        P(None, "dp", "mp"),
        P("mp", "dp"),
        P("dp", "mp"),
        P("mp", "dp"),
        P(),
        P(),
        P("dp", None, "mp", None),
    )
    out_specs = (P("dp", None, "mp", None), P())
    return jax.shard_map(
        on_device, mesh=mesh, in_specs=in_specs, out_specs=out_specs, check_vma=False
    )
```
